32 devices in a mesh: ctx: 16 (over z, x, core), dp: 2 (over y).
Axes of the slice: x: 2, y: 2, z: 4, core: 2. Of those that a mesh axis runs over, the one named last changes fastest.
Arguments:
- proj: bfloat16 [2, 2048, 1536], P('dp', 'ctx'), may hold values from -6 to 6
- short_filter: float32 [3, 1536], replicated, may hold values from -2.5 to 2.5
- long_filter: float32 [512, 2048], P('ctx'), may hold values from -1 to 1
- w_out: bfloat16 [512, 2048], P('ctx'), may hold values from -0.25 to 0.25
- dout: bfloat16 [2, 2048, 2048], P('dp', 'ctx'), may hold values from -6 to 6
- lengths: int32 [2], replicated, may hold values from 1024 to 2048, as said below
- counts: int32 [2], replicated, may hold values from 256 to 2048
Outputs:
- output: bfloat16 [2, 2048, 2048], P('dp', 'ctx')
- d_proj: bfloat16 [2, 2048, 1536], P('dp', 'ctx')
- d_wout: float32 [512, 2048], P('ctx')
- d_filter: float32 [512, 2048], P('ctx')
The draws below stay inside these ranges and needn't reach their ends.
Inputs may be any that keep to these rules, and one draw needn't show every extreme that they name: `lengths`: at least one sequence has the full length 2048.
All inputs are finite; a program needn't handle non-finite values.
Results may differ from the reference program's by a relative error of at most 0.0075.
Values may be sent and summed in bfloat16 or wider, within the bound.
No kernel may reach another device: no remote copies, remote signals or barrier semaphores. Data moves between devices by JAX's collectives and lax.ppermute only.
A program may use at most 64 MiB of HBM per device.

```python
import math
import jax
import jax.numpy as jnp

C = 512
D_OUT = 2048
TAPS = 3
SEQUENCE_LENGTH = 2048
BATCH = 2


def draw_long_filter(key, part):
    key = jax.random.fold_in(key, 11)
    decay_rate_key, spike_key, dropout_key, jitter_key = jax.random.split(key, 4)
    log_rate = jax.random.uniform(decay_rate_key, (C, 1), minval=math.log(30.0), maxval=math.log(4.0 * SEQUENCE_LENGTH))
    horizon = jnp.exp(log_rate)
    position_grid = jnp.arange(SEQUENCE_LENGTH, dtype=jnp.int32)
    spike_events = jax.random.randint(spike_key, (4,), 1, SEQUENCE_LENGTH)
    dropout_flags = jax.random.uniform(dropout_key, (C, 4), minval=0.5, maxval=0.8)
    decay_profile = jnp.exp(-position_grid.astype(jnp.float32)[None, :] / horizon)
    for spike_index in range(4):
        kept_entries = position_grid[None, :] >= spike_events[spike_index]
        decay_profile = decay_profile * jnp.where(kept_entries, dropout_flags[:, spike_index:spike_index + 1], 1.0)
    amplitude = 1.0 / jnp.sqrt(jnp.minimum(horizon, float(SEQUENCE_LENGTH)))
    noise = jax.random.truncated_normal(jitter_key, -4.0, 4.0, (C, SEQUENCE_LENGTH))
    return (noise * decay_profile * amplitude * 0.2).astype(jnp.float32)


def draw_lengths(key, part):
    key = jax.random.fold_in(key, 5)
    length_key, full_key = jax.random.split(key, 2)
    drawn = jax.random.randint(length_key, (BATCH,), SEQUENCE_LENGTH // 2, SEQUENCE_LENGTH + 1)
    full_index = jax.random.randint(full_key, (), 0, BATCH)
    member = jnp.arange(BATCH, dtype=jnp.int32)
    return jnp.where(member == full_index, SEQUENCE_LENGTH, drawn).astype(jnp.int32)


def block_scale(stream_key, shape, cuts, smallest, top_value):
    def one(dim, blocks):
        draws = jax.random.uniform(jax.random.fold_in(jax.random.fold_in(stream_key, 6), dim), (blocks,), jnp.float32, smallest / len(cuts), top_value / len(cuts))
        return jnp.repeat(jnp.exp(draws), shape[dim] // blocks).reshape((-1,) + (1,) * (len(shape) - dim - 1))

    factor_of = one(*cuts[0])
    for cut in cuts[1:]:
        factor_of = factor_of * one(*cut)
    return factor_of


def centred(rng, extent, spread, reach, cuts=(), held_as=jnp.bfloat16):
    loudness = block_scale(rng, extent, cuts, -0.22, 0.18) if cuts else 1.0
    values = jax.random.normal(rng, extent, jnp.float32) * spread * loudness
    return jnp.minimum(jnp.maximum(values, -reach), reach).astype(held_as)


def setup_inputs(seed: int = 0) -> dict:
    seeds = jax.random.split(jax.random.key(seed), 8)
    return {
        "proj": centred(seeds[0], (BATCH, SEQUENCE_LENGTH, 3 * C), 1.0, 6.0, ((0, 2), (1, 16))),
        "short_filter": centred(seeds[1], (TAPS, 3 * C), 0.7, 2.5, (), jnp.float32),
        "long_filter": draw_long_filter(jax.random.fold_in(seeds[7], 71), 0),
        "w_out": centred(seeds[3], (C, D_OUT), C ** -0.5, 0.25, ((0, 16),)),
        "dout": centred(seeds[4], (BATCH, SEQUENCE_LENGTH, D_OUT), 1.0, 6.0, ((0, 2), (1, 16))),
        "lengths": draw_lengths(jax.random.fold_in(seeds[7], 71), 0),
        "counts": jax.random.randint(seeds[6], (BATCH,), SEQUENCE_LENGTH // 8, SEQUENCE_LENGTH + 1).astype(jnp.int32),
    }


def conv_fft(signal, kernel):
    fft_size = 2 * signal.shape[1]
    spectra = jnp.fft.rfft(signal, n=fft_size) * jnp.fft.rfft(kernel, n=fft_size)
    return jnp.fft.irfft(spectra, n=fft_size)[:, :signal.shape[1]]

def corr_fft(kernel, signal):
    fft_size = 2 * signal.shape[1]
    spectra = jnp.conj(jnp.fft.rfft(kernel, n=fft_size)) * jnp.fft.rfft(signal, n=fft_size)
    return jnp.fft.irfft(spectra, n=fft_size)[:, :signal.shape[1]]

def reference(proj, short_filter, long_filter, w_out, dout, lengths, counts):
    count_float = counts.astype(jnp.float32)
    weights = count_float * BATCH / jnp.sum(count_float)
    grad_scale = 1.0 / math.sqrt(BATCH * SEQUENCE_LENGTH)
    position_grid = jnp.arange(SEQUENCE_LENGTH, dtype=jnp.int32)
    d_wout = jnp.zeros((C, D_OUT), jnp.float32)
    d_filter = jnp.zeros((C, SEQUENCE_LENGTH), jnp.float32)
    outputs = []
    grads = []
    for sample in range(BATCH):
        mask = (position_grid < lengths[sample]).astype(jnp.float32)[:, None]
        masked = proj[sample].astype(jnp.float32) * mask
        mixed = sum((short_filter[tap_index] * jnp.pad(masked, ((tap_index, 0), (0, 0)))[:SEQUENCE_LENGTH] for tap_index in range(TAPS)))
        query_part = mixed[:, :C]
        key_part = mixed[:, C:2 * C]
        value_part = mixed[:, 2 * C:]
        gated = (key_part * value_part).astype(jnp.bfloat16)
        long_out = conv_fft(gated.astype(jnp.float32).T, long_filter).T.astype(jnp.bfloat16)
        long_float = long_out.astype(jnp.float32)
        product = (query_part * long_float).astype(jnp.bfloat16)
        outputs.append(jnp.dot(product, w_out, preferred_element_type=jnp.float32).astype(jnp.bfloat16))
        cotangent = (dout[sample].astype(jnp.float32) * mask * weights[sample]).astype(jnp.bfloat16)
        d_product = jnp.dot(cotangent, w_out.T, preferred_element_type=jnp.float32)
        d_wout = d_wout + grad_scale * jnp.dot(product.T, cotangent, preferred_element_type=jnp.float32)
        d_query = d_product * long_float
        d_long = (d_product * query_part).astype(jnp.bfloat16)
        d_long_cols = d_long.astype(jnp.float32).T
        d_gated = corr_fft(long_filter, d_long_cols).T.astype(jnp.bfloat16).astype(jnp.float32)
        d_filter = d_filter + grad_scale * corr_fft(gated.astype(jnp.float32).T, d_long_cols)
        d_mixed = jnp.concatenate([d_query, d_gated * value_part, d_gated * key_part], axis=1)
        d_masked = sum((short_filter[tap_index] * jnp.pad(d_mixed, ((0, tap_index), (0, 0)))[tap_index:] for tap_index in range(TAPS)))
        grads.append((d_masked * mask).astype(jnp.bfloat16))
    return (jnp.stack(outputs), jnp.stack(grads), d_wout, d_filter)
```

```python
import functools
import math

import jax
import jax.numpy as jnp
import ml_dtypes
import numpy as np
from jax import lax
from jax.experimental import pallas as pl
from jax.experimental.pallas import tpu as pltpu
from jax.sharding import Mesh
from jax.sharding import PartitionSpec as P

F32 = jnp.float32
BF16 = jnp.bfloat16
LANES = 128
VMEM = pl.BlockSpec(memory_space=pltpu.VMEM)
SMEM = pl.BlockSpec(memory_space=pltpu.SMEM)


def split_bf16(values):
    high = values.astype(ml_dtypes.bfloat16)
    low = (values - high.astype(np.float64)).astype(ml_dtypes.bfloat16)
    return high, low


def fft_tables(blocks):
    size = 2 * blocks * LANES
    k1 = np.arange(blocks + 1)[:, None]
    lane = np.arange(LANES)
    angle = -2.0 * np.pi * (k1 * lane[None, :] % size) / size
    twist = np.stack([np.cos(angle), np.sin(angle)]).astype(np.float32)
    inner = -2.0 * np.pi * (lane[:, None] * lane[None, :] % LANES) / LANES
    cos, sin = np.cos(inner), np.sin(inner)
    matrix = np.block([[cos, sin], [-sin, cos]])
    high, low = split_bf16(matrix)
    return jnp.asarray(twist), jnp.asarray(high), jnp.asarray(low)


def real_fft(values):
    half = len(values)
    if half == 1:
        return [(values[0], None), (values[0], None)]
    even, odd = real_fft(values[0::2]), real_fft(values[1::2])
    out = [None] * (half + 1)
    out[0] = (even[0][0] + odd[0][0], None)
    out[half] = (even[0][0] - odd[0][0], None)
    out[half // 2] = (even[half // 2][0], -odd[half // 2][0])
    for k in range(1, half // 2):
        cos, sin = math.cos(math.pi * k / half), -math.sin(math.pi * k / half)
        (e_re, e_im), (o_re, o_im) = even[k], odd[k]
        t_re = o_re * cos - o_im * sin
        t_im = o_re * sin + o_im * cos
        out[k] = (e_re + t_re, e_im + t_im)
        out[half - k] = (e_re - t_re, t_im - e_im)
    return out


def real_ifft(spectrum):
    half = len(spectrum) - 1
    if half == 1:
        return [spectrum[0][0] + spectrum[1][0]]
    even = [None] * (half // 2 + 1)
    odd = [None] * (half // 2 + 1)
    even[0] = (spectrum[0][0] + spectrum[half][0], None)
    odd[0] = (spectrum[0][0] - spectrum[half][0], None)
    even[half // 2] = (2.0 * spectrum[half // 2][0], None)
    odd[half // 2] = (-2.0 * spectrum[half // 2][1], None)
    for k in range(1, half // 2):
        cos, sin = math.cos(math.pi * k / half), math.sin(math.pi * k / half)
        (a_re, a_im), (b_re, b_im) = spectrum[k], spectrum[half - k]
        even[k] = (a_re + b_re, a_im - b_im)
        d_re, d_im = a_re - b_re, a_im + b_im
        odd[k] = (d_re * cos - d_im * sin, d_re * sin + d_im * cos)
    out = [None] * half
    out[0::2] = real_ifft(even)
    out[1::2] = real_ifft(odd)
    return out


def split_dot(left, high, low, transposed):
    dims = (((1,), (1 if transposed else 0,)), ((), ()))
    dot = functools.partial(lax.dot_general, dimension_numbers=dims, preferred_element_type=F32)
    left_high = left.astype(BF16)
    left_low = (left - left_high.astype(F32)).astype(BF16)
    return dot(left_high, high) + (dot(left_low, high) + dot(left_high, low))


def to_spectrum(load, blocks, chans, twist, high, low, work):
    for first in range(0, chans, 8):
        rows = slice(first, first + 8)
        freqs = real_fft([load(n1, rows) for n1 in range(blocks)])
        for k1, (re, im) in enumerate(freqs):
            at = slice(k1 * chans + first, k1 * chans + first + 8)
            if k1 == 0:
                work[at, :LANES] = re
                work[at, LANES:] = jnp.zeros_like(re)
                continue
            cos, sin = twist[0, k1 : k1 + 1, :], twist[1, k1 : k1 + 1, :]
            if im is None:
                work[at, :LANES] = re * cos
                work[at, LANES:] = re * sin
            else:
                work[at, :LANES] = re * cos - im * sin
                work[at, LANES:] = re * sin + im * cos
    return split_dot(work[...], high[...], low[...], False)


def from_spectrum(spectrum, blocks, chans, twist, high, low, work, store):
    scale = 1.0 / (2 * blocks * LANES)
    work[...] = split_dot(spectrum, high[...], low[...], True)
    for first in range(0, chans, 8):
        rows = slice(first, first + 8)
        freqs = []
        for k1 in range(blocks + 1):
            at = slice(k1 * chans + first, k1 * chans + first + 8)
            re, im = work[at, :LANES] * scale, work[at, LANES:] * scale
            cos, sin = twist[0, k1 : k1 + 1, :], twist[1, k1 : k1 + 1, :]
            if k1 == 0:
                freqs.append((re, None))
            elif k1 == blocks:
                freqs.append((re * cos + im * sin, None))
            else:
                freqs.append((re * cos + im * sin, im * cos - re * sin))
        for n1, value in enumerate(real_ifft(freqs)):
            store(n1, rows, value)


def times(a, b):
    a_re, a_im, b_re, b_im = a[:, :LANES], a[:, LANES:], b[:, :LANES], b[:, LANES:]
    return jnp.concatenate([a_re * b_re - a_im * b_im, a_re * b_im + a_im * b_re], axis=1)


def conj_times(a, b):
    a_re, a_im, b_re, b_im = a[:, :LANES], a[:, LANES:], b[:, :LANES], b[:, LANES:]
    return jnp.concatenate([a_re * b_re + a_im * b_im, a_re * b_im - a_im * b_re], axis=1)


def filter_kernel(filt, twist, high, low, spec, work, *, blocks, chans):
    def load(n1, rows):
        return filt[rows, n1 * LANES : (n1 + 1) * LANES]

    spec[...] = to_spectrum(load, blocks, chans, twist, high, low, work)


def forward_kernel(
    gated, filt_spec, twist, high, low, long_out, gated_spec, work, signal, *, blocks, chans
):
    for n1 in range(blocks):
        signal[n1] = gated[n1].astype(F32)

    def load(n1, rows):
        return signal[n1, rows, :]

    spec = to_spectrum(load, blocks, chans, twist, high, low, work)
    gated_spec[...] = spec

    def store(n1, rows, value):
        signal[n1, rows, :] = value

    from_spectrum(times(spec, filt_spec[...]), blocks, chans, twist, high, low, work, store)
    for n1 in range(blocks):
        long_out[n1] = signal[n1].astype(BF16)


def backward_kernel(
    d_long,
    filt_spec,
    gated_spec,
    twist,
    high,
    low,
    d_gated,
    d_filter,
    work,
    signal,
    held,
    *,
    blocks,
    chans,
    scale,
):
    for n1 in range(blocks):
        signal[n1] = d_long[n1].astype(F32)

    def load(n1, rows):
        return signal[n1, rows, :]

    held[...] = to_spectrum(load, blocks, chans, twist, high, low, work)

    def store(n1, rows, value):
        signal[n1, rows, :] = value

    spec = conj_times(filt_spec[...], held[...])
    from_spectrum(spec, blocks, chans, twist, high, low, work, store)
    for n1 in range(blocks):
        d_gated[n1] = signal[n1].astype(BF16)
    spec = conj_times(gated_spec[...], held[...])
    from_spectrum(spec, blocks, chans, twist, high, low, work, store)
    for n1 in range(blocks):
        d_filter[:, n1 * LANES : (n1 + 1) * LANES] = (signal[n1] * scale).astype(BF16)


def prep_kernel(ints, proj, earlier, taps, gated_t, query_t, key_t, value_t, *, width):
    rows = proj.shape[0]
    start, length = ints[2], ints[3]
    position = start + lax.broadcasted_iota(jnp.int32, (rows, 1), 0)
    keep = position < length
    row = lax.broadcasted_iota(jnp.int32, (rows, 1), 0)
    streams = []
    for stream in range(3):
        cols = slice(stream * width, (stream + 1) * width)
        masked = jnp.where(keep, proj[:, cols].astype(F32), 0.0)
        past = earlier[:, cols].astype(F32)
        mixed = taps[0:1, cols] * masked
        for tap in range(1, 3):
            shifted = pltpu.roll(masked, tap, 0)
            for r in range(tap):
                shifted = jnp.where(row == r, past[2 - tap + r : 3 - tap + r, :], shifted)
            mixed = mixed + taps[tap : tap + 1, cols] * shifted
        streams.append(mixed)
    gated_t[...] = (streams[1] * streams[2]).T.astype(BF16)
    query_t[...] = streams[0].T
    key_t[...] = streams[1].T
    value_t[...] = streams[2].T


def natural_row(ints, rel_h, rel_c, line, shape):
    h = (ints[0] + rel_h) % 2
    c = (ints[1] + rel_c) % 2
    lines, chans, line_first = shape
    place = (line * 2 + h) * 2 + c if line_first else (h * lines + line) * 2 + c
    return pl.multiple_of(place * chans, chans)


PIECES = ((0, 0), (1, 0), (0, 1), (1, 1))


def piece_rows(refs, piece):
    near, over, across = refs
    if piece == 0:
        return near[...]
    if piece == 1:
        return over[...]
    return across[piece - 2]


def d_long_kernel(
    ints, floats, dout, near, over, across, query_t, cot, d_product_t, d_long_t, *, shape
):
    lines, chans, _ = shape
    rows = dout.shape[0]
    position = ints[2] + lax.broadcasted_iota(jnp.int32, (rows, 1), 0)
    mask = jnp.where(position < ints[3], 1.0, 0.0)
    cot[...] = (dout[...].astype(F32) * mask * floats[0]).astype(BF16)
    for piece, (rel_h, rel_c) in enumerate(PIECES):
        got = lax.dot_general(
            piece_rows((near, over, across), piece),
            cot[...],
            (((1,), (1,)), ((), ())),
            preferred_element_type=F32,
        )
        for line in range(lines):
            at = natural_row(ints, rel_h, rel_c, line, shape)
            d_product_t[pl.ds(at, chans), :] = got[line * chans : (line + 1) * chans]
    d_long_t[...] = (d_product_t[...] * query_t[...]).astype(BF16)


def partial_kernel(
    ints, long_t, query_t, cot, product, send, stay, product_t, *, shape, scale, tile
):
    lines, chans, _ = shape
    product_t[...] = query_t[...] * long_t[...].astype(F32)
    for piece, (rel_h, rel_c) in enumerate(PIECES):
        left = jnp.concatenate(
            [
                product_t[pl.ds(natural_row(ints, rel_h, rel_c, line, shape), chans), :]
                for line in range(lines)
            ],
            axis=0,
        )
        product[piece] = left.T.astype(BF16)
        left = left.astype(BF16)
        for first in range(0, cot.shape[1], tile):
            cols = slice(first, first + tile)
            got = jnp.dot(left, cot[:, cols], preferred_element_type=F32) * scale
            if rel_c:
                send[rel_h, :, cols] = got.astype(BF16)
            else:
                stay[rel_h, :, cols] = got


def output_kernel(product, near, over, across, out, *, tile):
    for first in range(0, out.shape[1], tile):
        cols = slice(first, first + tile)
        total = jnp.dot(product[0], near[:, cols], preferred_element_type=F32)
        total += jnp.dot(product[1], over[:, cols], preferred_element_type=F32)
        total += jnp.dot(product[2], across[0, :, cols], preferred_element_type=F32)
        total += jnp.dot(product[3], across[1, :, cols], preferred_element_type=F32)
        out[:, cols] = total.astype(BF16)


def mixed_grad_kernel(d_product_t, long_t, d_gated_t, key_t, value_t, d_mixed, *, width):
    d_gated = d_gated_t[...].astype(F32)
    d_mixed[:, :width] = (d_product_t[...] * long_t[...].astype(F32)).T
    d_mixed[:, width : 2 * width] = (d_gated * value_t[...]).T
    d_mixed[:, 2 * width :] = (d_gated * key_t[...]).T


def proj_grad_kernel(ints, d_mixed, later, taps, d_proj):
    rows = d_mixed.shape[0]
    row = lax.broadcasted_iota(jnp.int32, (rows, 1), 0)
    keep = ints[2] + row < ints[3]
    total = taps[0:1, :] * d_mixed[...]
    for tap in range(1, 3):
        shifted = pltpu.roll(d_mixed[...], rows - tap, 0)
        for r in range(tap):
            shifted = jnp.where(row == rows - tap + r, later[r : r + 1, :], shifted)
        total = total + taps[tap : tap + 1, :] * shifted
    d_proj[...] = jnp.where(keep, total, 0.0).astype(BF16)


def call(kernel, outs, specs, scratch=(), flops=0, moved=1 << 20):
    return pl.pallas_call(
        kernel,
        out_shape=[jax.ShapeDtypeStruct(s, d) for s, d in outs],
        in_specs=specs,
        out_specs=[VMEM] * len(outs),
        scratch_shapes=list(scratch),
        compiler_params=pltpu.CompilerParams(vmem_limit_bytes=40 << 20),
        cost_estimate=pl.CostEstimate(flops=flops, bytes_accessed=moved, transcendentals=0),
    )


CTX = None
SWAP = ((0, 1), (1, 0))


def swap(block, axis):
    return lax.ppermute(block, axis, SWAP)


def dp_sum(block):
    if lax.axis_size("dp") == 2:
        return block.astype(F32) + swap(block, "dp").astype(F32)
    return lax.psum(block, "dp").astype(F32)


def per_device(axes, proj, short_filter, long_filter, w_out, dout, lengths, counts):
    rows, width = proj.shape[1], proj.shape[2] // 3
    chans, seq_len = long_filter.shape
    features = w_out.shape[1]
    batch = lengths.shape[0]
    ctx_size = seq_len // rows
    lines = lax.axis_size("l")
    shape = (lines, chans, axes[0] == "l")
    grad_scale = 1.0 / math.sqrt(batch * seq_len)
    here = lax.axis_index(axes)
    samples = batch // lax.axis_size("dp")
    assert samples == 1
    picked = jnp.arange(batch, dtype=jnp.int32) == lax.axis_index("dp")
    length_here = jnp.sum(jnp.where(picked, lengths, 0))
    count_float = counts.astype(F32)
    weight_here = jnp.sum(jnp.where(picked, count_float, 0.0)) * batch / jnp.sum(count_float)
    ints = jnp.stack(
        [lax.axis_index("h"), lax.axis_index("c"), here * rows, length_here]
    ).astype(jnp.int32)
    floats = weight_here.reshape(1)

    near = lax.all_to_all(
        jnp.broadcast_to(w_out[None], (lines,) + w_out.shape), "l", 0, 0, tiled=True
    ).reshape(lines * chans, features)
    over = swap(near, "h")
    across = swap(jnp.stack([near, over]), "c")

    tail = proj[0, rows - 2 :]
    tail_at = here * rows + rows - 2 + jnp.arange(2, dtype=jnp.int32)
    tail = jnp.where((tail_at < length_here)[:, None], tail, jnp.zeros_like(tail))
    route = [(i, i + 1) for i in range(ctx_size - 1)]
    earlier = lax.ppermute(tail, axes, route)
    flat = (width, rows)
    gated_t, query_t, key_t, value_t = call(
        functools.partial(prep_kernel, width=width),
        [(flat, BF16), (flat, F32), (flat, F32), (flat, F32)],
        [SMEM] + [VMEM] * 3,
        flops=1 << 20,
    )(ints, proj[0], earlier, short_filter)

    def exchange(block):
        return lax.all_to_all(block, axes, 0, 0, tiled=True)

    blocked = (ctx_size, chans, rows)
    tables = fft_tables(ctx_size)
    spec_shape = ((ctx_size + 1) * chans, 2 * LANES)
    sizes = {"blocks": ctx_size, "chans": chans}
    work = pltpu.VMEM(spec_shape, F32)
    signal = pltpu.VMEM(blocked, F32)
    fft_flops = 6 * spec_shape[0] * 2 * LANES * 2 * LANES
    (filt_spec,) = call(
        functools.partial(filter_kernel, **sizes),
        [(spec_shape, F32)],
        [VMEM] * 4,
        [work],
        flops=fft_flops,
    )(long_filter, *tables)
    gated_cols = exchange(gated_t.reshape(blocked))
    long_cols, gated_spec = call(
        functools.partial(forward_kernel, **sizes),
        [(blocked, BF16), (spec_shape, F32)],
        [VMEM] * 5,
        [work, signal],
        flops=2 * fft_flops,
    )(gated_cols, filt_spec, *tables)
    long_t = exchange(long_cols).reshape(flat)

    cot, d_product_t, d_long_t = call(
        functools.partial(d_long_kernel, shape=shape),
        [((rows, features), BF16), (flat, F32), (flat, BF16)],
        [SMEM, SMEM] + [VMEM] * 5,
        flops=2 * rows * width * features,
        moved=4 << 20,
    )(ints, floats, dout[0], near, over, across, query_t)
    d_long_cols = exchange(d_long_t.reshape(blocked))
    d_gated_cols, filter_part = call(
        functools.partial(backward_kernel, scale=grad_scale, **sizes),
        [(blocked, BF16), ((chans, seq_len), BF16)],
        [VMEM] * 6,
        [work, signal, work],
        flops=3 * fft_flops,
    )(d_long_cols, filt_spec, gated_spec, *tables)
    d_gated_t = exchange(d_gated_cols).reshape(flat)
    d_filter = dp_sum(filter_part)

    part = (2, lines * chans, features)
    product, send, stay = call(
        functools.partial(partial_kernel, shape=shape, scale=grad_scale, tile=512),
        [((4, rows, lines * chans), BF16), (part, BF16), (part, F32)],
        [SMEM] + [VMEM] * 3,
        [pltpu.VMEM(flat, F32)],
        flops=2 * rows * width * features,
        moved=4 << 20,
    )(ints, long_t, query_t, cot)
    pair = stay + swap(send, "c").astype(F32)
    quad = pair[0] + swap(pair[1].astype(BF16), "h").astype(F32)
    row_sums = jnp.sum(
        lax.all_to_all(
            quad.astype(BF16).reshape(lines, chans, features), "l", 0, 0, tiled=True
        ).astype(F32),
        axis=0,
    )
    d_wout = dp_sum(row_sums.astype(BF16))

    (output,) = call(
        functools.partial(output_kernel, tile=512),
        [((rows, features), BF16)],
        [VMEM] * 4,
        flops=2 * rows * width * features,
        moved=4 << 20,
    )(product, near, over, across.reshape(2, lines * chans, features))

    (d_mixed,) = call(
        functools.partial(mixed_grad_kernel, width=width),
        [((rows, 3 * width), F32)],
        [VMEM] * 5,
        flops=1 << 20,
    )(d_product_t, long_t, d_gated_t, key_t, value_t)
    later = lax.ppermute(d_mixed[:2], axes, [(j, i) for i, j in route])
    (d_proj,) = call(
        proj_grad_kernel,
        [((rows, 3 * width), BF16)],
        [SMEM] + [VMEM] * 3,
        flops=1 << 20,
    )(ints, d_mixed, later, short_filter)
    return output[None], d_proj[None], d_wout, d_filter


def solution(mesh):
    ctx, dp = mesh.shape["ctx"], mesh.shape["dp"]
    if ctx == 16:
        axes, dims = ("l", "h", "c"), (4, 2, 2)
    else:
        axes, dims = ("h", "l", "c"), (2, ctx // 4, 2)
    fine = Mesh(mesh.devices.reshape(dims + (dp,)), axes + ("dp",))
    placed = (
        P("dp", axes, None),
        P(),
        P(axes, None),
        P(axes, None),
        P("dp", axes, None),
        P(),
        P(),
    )
    return jax.shard_map(
        functools.partial(per_device, axes),
        mesh=fine,
        in_specs=placed,
        out_specs=(P("dp", axes, None), P("dp", axes, None), P(axes, None), P(axes, None)),
        check_vma=False,
    )
```

```python
import functools
import math
import typing

import jax
import jax.numpy as jnp
import ml_dtypes
import numpy as np
from jax import lax
from jax.experimental import pallas as pl
from jax.experimental.pallas import tpu as pltpu
from jax.sharding import Mesh
from jax.sharding import PartitionSpec as P

F32 = jnp.float32
BF16 = jnp.bfloat16
LANES = 128
VMEM_LIMIT = 20 << 20
SMEM = pl.BlockSpec(memory_space=pltpu.SMEM)
HBM = pl.BlockSpec(memory_space=pltpu.HBM)


def split_bf16(values):
    high = values.astype(ml_dtypes.bfloat16)
    low = (values - high.astype(np.float64)).astype(ml_dtypes.bfloat16)
    return high, low


def fft_tables(blocks):
    size = 2 * blocks * LANES
    k1 = np.arange(blocks + 1)[:, None]
    lane = np.arange(LANES)
    angle = -2.0 * np.pi * (k1 * lane[None, :] % size) / size
    twist = np.stack([np.cos(angle), np.sin(angle)]).astype(np.float32)
    inner = -2.0 * np.pi * (lane[:, None] * lane[None, :] % LANES) / LANES
    cos, sin = np.cos(inner), np.sin(inner)
    matrix = np.block([[cos, sin], [-sin, cos]])
    high, low = split_bf16(matrix)
    return jnp.asarray(twist), jnp.asarray(np.stack([high, low]))


def real_fft(values):
    half = len(values)
    if half == 1:
        return [(values[0], None), (values[0], None)]
    even, odd = real_fft(values[0::2]), real_fft(values[1::2])
    out = [None] * (half + 1)
    out[0] = (even[0][0] + odd[0][0], None)
    out[half] = (even[0][0] - odd[0][0], None)
    out[half // 2] = (even[half // 2][0], -odd[half // 2][0])
    for k in range(1, half // 2):
        cos, sin = math.cos(math.pi * k / half), -math.sin(math.pi * k / half)
        (e_re, e_im), (o_re, o_im) = even[k], odd[k]
        t_re = o_re * cos - o_im * sin
        t_im = o_re * sin + o_im * cos
        out[k] = (e_re + t_re, e_im + t_im)
        out[half - k] = (e_re - t_re, t_im - e_im)
    return out


def real_ifft(spectrum):
    half = len(spectrum) - 1
    if half == 1:
        return [spectrum[0][0] + spectrum[1][0]]
    even = [None] * (half // 2 + 1)
    odd = [None] * (half // 2 + 1)
    even[0] = (spectrum[0][0] + spectrum[half][0], None)
    odd[0] = (spectrum[0][0] - spectrum[half][0], None)
    even[half // 2] = (2.0 * spectrum[half // 2][0], None)
    odd[half // 2] = (-2.0 * spectrum[half // 2][1], None)
    for k in range(1, half // 2):
        cos, sin = math.cos(math.pi * k / half), math.sin(math.pi * k / half)
        (a_re, a_im), (b_re, b_im) = spectrum[k], spectrum[half - k]
        even[k] = (a_re + b_re, a_im - b_im)
        d_re, d_im = a_re - b_re, a_im + b_im
        odd[k] = (d_re * cos - d_im * sin, d_re * sin + d_im * cos)
    out = [None] * half
    out[0::2] = real_ifft(even)
    out[1::2] = real_ifft(odd)
    return out


def split_dot(left, high, low, transposed):
    dims = (((1,), (1 if transposed else 0,)), ((), ()))
    dot = functools.partial(lax.dot_general, dimension_numbers=dims, preferred_element_type=F32)
    left_high = left.astype(BF16)
    left_low = (left - left_high.astype(F32)).astype(BF16)
    return dot(left_high, high) + (dot(left_low, high) + dot(left_high, low))


def to_spectrum(load, blocks, chans, twist, matrix, work):
    for first in range(0, chans, 8):
        rows = slice(first, first + 8)
        freqs = real_fft([load(n1, rows) for n1 in range(blocks)])
        for k1, (re, im) in enumerate(freqs):
            at = slice(k1 * chans + first, k1 * chans + first + 8)
            if k1 == 0:
                work[at, :LANES] = re
                work[at, LANES:] = jnp.zeros_like(re)
                continue
            cos, sin = twist[0, k1 : k1 + 1, :], twist[1, k1 : k1 + 1, :]
            if im is None:
                work[at, :LANES] = re * cos
                work[at, LANES:] = re * sin
            else:
                work[at, :LANES] = re * cos - im * sin
                work[at, LANES:] = re * sin + im * cos
    return split_dot(work[...], matrix[0], matrix[1], False)


def from_spectrum(spectrum, blocks, chans, twist, matrix, work, store):
    scale = 1.0 / (2 * blocks * LANES)
    work[...] = split_dot(spectrum, matrix[0], matrix[1], True)
    for first in range(0, chans, 8):
        rows = slice(first, first + 8)
        freqs = []
        for k1 in range(blocks + 1):
            at = slice(k1 * chans + first, k1 * chans + first + 8)
            re, im = work[at, :LANES] * scale, work[at, LANES:] * scale
            cos, sin = twist[0, k1 : k1 + 1, :], twist[1, k1 : k1 + 1, :]
            if k1 == 0:
                freqs.append((re, None))
            elif k1 == blocks:
                freqs.append((re * cos + im * sin, None))
            else:
                freqs.append((re * cos + im * sin, im * cos - re * sin))
        for n1, value in enumerate(real_ifft(freqs)):
            store(n1, rows, value)


def times(a, b):
    a_re, a_im, b_re, b_im = a[:, :LANES], a[:, LANES:], b[:, :LANES], b[:, LANES:]
    return jnp.concatenate([a_re * b_re - a_im * b_im, a_re * b_im + a_im * b_re], axis=1)


def conj_times(a, b):
    a_re, a_im, b_re, b_im = a[:, :LANES], a[:, LANES:], b[:, :LANES], b[:, LANES:]
    return jnp.concatenate([a_re * b_re + a_im * b_im, a_re * b_im - a_im * b_re], axis=1)


def filter_kernel(filt, twist, matrix, spec, work, *, blocks, chans):
    def load(n1, rows):
        return filt[rows, n1 * LANES : (n1 + 1) * LANES]

    spec[...] = to_spectrum(load, blocks, chans, twist, matrix, work)


def forward_kernel(
    gated, filt_spec, twist, matrix, long_out, gated_spec, work, signal, *, blocks, chans
):
    for n1 in range(blocks):
        signal[n1] = gated[n1].astype(F32)

    def load(n1, rows):
        return signal[n1, rows, :]

    spec = to_spectrum(load, blocks, chans, twist, matrix, work)
    gated_spec[...] = spec

    def store(n1, rows, value):
        signal[n1, rows, :] = value

    from_spectrum(times(spec, filt_spec[...]), blocks, chans, twist, matrix, work, store)
    for n1 in range(blocks):
        long_out[n1] = signal[n1].astype(BF16)


def backward_kernel(
    d_long,
    filt_spec,
    gated_spec,
    twist,
    matrix,
    d_gated,
    d_filter,
    work,
    signal,
    held,
    *,
    blocks,
    chans,
    scale,
):
    for n1 in range(blocks):
        signal[n1] = d_long[n1].astype(F32)

    def load(n1, rows):
        return signal[n1, rows, :]

    held[...] = to_spectrum(load, blocks, chans, twist, matrix, work)

    def store(n1, rows, value):
        signal[n1, rows, :] = value

    spec = conj_times(filt_spec[...], held[...])
    from_spectrum(spec, blocks, chans, twist, matrix, work, store)
    for n1 in range(blocks):
        d_gated[n1] = signal[n1].astype(BF16)
    spec = conj_times(gated_spec[...], held[...])
    from_spectrum(spec, blocks, chans, twist, matrix, work, store)
    for n1 in range(blocks):
        d_filter[:, n1 * LANES : (n1 + 1) * LANES] = (signal[n1] * scale).astype(BF16)


class Split(typing.NamedTuple):
    samples: int
    lines: int
    chans: int
    line_first: bool


def mixed_stream(stream, proj, earlier, taps, room, width):
    rows = proj.shape[0]
    row = lax.broadcasted_iota(jnp.int32, (rows, 1), 0)
    past_row = lax.broadcasted_iota(jnp.int32, (2, 1), 0)
    cols = slice(stream * width, (stream + 1) * width)
    masked = jnp.where(row < room, proj[:, cols].astype(F32), 0.0)
    past = jnp.where(past_row < room + 2, earlier[:, cols].astype(F32), 0.0)
    mixed = taps[0:1, cols] * masked
    for tap in range(1, 3):
        shifted = pltpu.roll(masked, tap, 0)
        for r in range(tap):
            shifted = jnp.where(row == r, past[2 - tap + r : 3 - tap + r, :], shifted)
        mixed = mixed + taps[tap : tap + 1, cols] * shifted
    return mixed


def prep_kernel(
    scalars, proj_far, earlier, taps_far, gated_t, query_t, proj, taps, done, *, width, split
):
    copies = [
        pltpu.make_async_copy(proj_far, proj, done.at[0]),
        pltpu.make_async_copy(taps_far, taps, done.at[1]),
    ]
    for copy in copies:
        copy.start()
    for copy in copies:
        copy.wait()
    room = room_left(scalars, split, proj.shape[0])
    query, key, value = (
        mixed_stream(stream, proj, earlier, taps, room, width) for stream in range(3)
    )
    gated_t[...] = (key * value).T.astype(BF16)
    query_t[...] = query.T


def room_left(scalars, split, rows):
    group, sample = scalars[0] // split.samples, scalars[0] % split.samples
    length = scalars[1]
    for other in range(1, split.samples):
        length = jnp.where(sample == other, scalars[1 + other], length)
    return length - group * rows


def loss_weight(scalars, split):
    sample = scalars[0] % split.samples
    total, mine = jnp.float32(0), jnp.float32(0)
    for other in range(split.samples):
        count = scalars[1 + split.samples + other].astype(F32)
        total = total + count
        mine = jnp.where(sample == other, count, mine)
    return jnp.full((1, LANES), mine * split.samples) / jnp.full((1, LANES), total)


def natural_row(scalars, rel_h, rel_c, step, split):
    group = scalars[0] // split.samples
    lines, chans = split.lines, split.chans
    c = (group % 2 + rel_c) % 2
    if split.line_first:
        h, line = group // 2 % 2, group // 4
    else:
        h, line = group // (2 * lines), group // 2 % lines
    h, line = (h + rel_h) % 2, (line + lines - step) % lines
    at = (line * 2 + h) * 2 + c if split.line_first else (h * lines + line) * 2 + c
    return pl.multiple_of(at * chans, chans)


PIECES = ((0, 0), (1, 0), (0, 1), (1, 1))
CHUNKS = 1


def cotangent_kernel(scalars, dout, cot, *, split):
    rows = dout.shape[0]
    row = lax.broadcasted_iota(jnp.int32, (rows, 1), 0)
    mask = jnp.where(row < room_left(scalars, split, rows), 1.0, 0.0)
    weight = loss_weight(scalars, split)[:, :1]
    cot[...] = (dout[...].astype(F32) * mask * weight).astype(BF16)


def d_long_kernel(scalars, cot, query_t, *refs, split):
    *weights, d_product_t, d_long_t = refs
    lines, chans = split.lines, split.chans
    part = cot.shape[1] // CHUNKS
    for piece, (rel_h, rel_c) in enumerate(PIECES):
        got = sum(
            lax.dot_general(
                weights[piece * CHUNKS + chunk][...],
                cot[:, chunk * part : (chunk + 1) * part],
                (((1,), (1,)), ((), ())),
                preferred_element_type=F32,
            )
            for chunk in range(CHUNKS)
        )
        for line in range(lines):
            at = natural_row(scalars, rel_h, rel_c, line, split)
            d_product_t[pl.ds(at, chans), :] = got[line * chans : (line + 1) * chans]
    d_long_t[...] = (d_product_t[...] * query_t[...]).astype(BF16)


def partial_kernel(
    scalars, long_t, query_t, cot, product, *refs, split, scale, tile
):
    *parts, product_t = refs
    lines, chans = split.lines, split.chans
    part = cot.shape[1] // CHUNKS
    product_t[...] = query_t[...] * long_t[...].astype(F32)
    for piece, (rel_h, rel_c) in enumerate(PIECES):
        left = jnp.concatenate(
            [
                product_t[pl.ds(natural_row(scalars, rel_h, rel_c, line, split), chans), :]
                for line in range(lines)
            ],
            axis=0,
        )
        product[piece] = left.T.astype(BF16)
        left = left.astype(BF16)
        for first in range(0, cot.shape[1], tile):
            cols = slice(first, first + tile)
            got = jnp.dot(left, cot[:, cols], preferred_element_type=F32) * scale
            out = parts[(2 * rel_c + rel_h) * CHUNKS + first // part]
            out[:, first % part : first % part + tile] = got.astype(BF16)


def output_kernel(product, *refs, tile):
    *weights, out = refs
    part = out.shape[1] // CHUNKS
    for first in range(0, out.shape[1], tile):
        chunk, cols = first // part, slice(first % part, first % part + tile)
        total = sum(
            jnp.dot(
                product[piece], weights[piece * CHUNKS + chunk][:, cols], preferred_element_type=F32
            )
            for piece in range(4)
        )
        out[:, first : first + tile] = total.astype(BF16)


def mixed_grads(d_product_t, long_t, d_gated_t, key, value, rows):
    d_query = (d_product_t[...] * long_t[...].astype(F32)).T[:rows]
    d_gated = d_gated_t[...].astype(F32).T[:rows]
    return d_query, d_gated * value[:rows], d_gated * key[:rows]


def head_kernel(
    scalars, proj, earlier, taps, d_product_t, long_t, d_gated_t, head, *, width, split
):
    room = room_left(scalars, split, proj.shape[0])
    key, value = (mixed_stream(i, proj, earlier, taps, room, width) for i in (1, 2))
    grads = mixed_grads(d_product_t, long_t, d_gated_t, key, value, 8)
    for stream, grad in enumerate(grads):
        head[:, stream * width : (stream + 1) * width] = grad


def proj_grad_kernel(
    scalars,
    proj,
    earlier,
    taps,
    d_product_t,
    long_t,
    d_gated_t,
    later,
    d_proj,
    *,
    width,
    split,
):
    rows = proj.shape[0]
    row = lax.broadcasted_iota(jnp.int32, (rows, 1), 0)
    room = room_left(scalars, split, rows)
    key, value = (mixed_stream(i, proj, earlier, taps, room, width) for i in (1, 2))
    grads = mixed_grads(d_product_t, long_t, d_gated_t, key, value, rows)
    for stream, grad in enumerate(grads):
        cols = slice(stream * width, (stream + 1) * width)
        total = taps[0:1, cols] * grad
        for tap in range(1, 3):
            shifted = pltpu.roll(grad, rows - tap, 0)
            for r in range(tap):
                shifted = jnp.where(row == rows - tap + r, later[r : r + 1, cols], shifted)
            total = total + taps[tap : tap + 1, cols] * shifted
        d_proj[:, cols] = jnp.where(row < room, total, 0.0).astype(BF16)


def call(kernel, outs, args, scalars=0, scratch=(), flops=0, far=()):
    def full(value):
        return pl.BlockSpec(value.shape, lambda i, n=len(value.shape): (0,) * n)

    out_shape = [jax.ShapeDtypeStruct(shape, dtype) for shape, dtype in outs]
    return pl.pallas_call(
        kernel,
        grid=(1,),
        out_shape=out_shape,
        in_specs=[
            SMEM if i < scalars else HBM if i in far else full(v) for i, v in enumerate(args)
        ],
        out_specs=[full(v) for v in out_shape],
        scratch_shapes=list(scratch),
        compiler_params=pltpu.CompilerParams(vmem_limit_bytes=VMEM_LIMIT),
        cost_estimate=pl.CostEstimate(flops=flops, bytes_accessed=1024, transcendentals=0),
    )(*args)


SWAP = ((0, 1), (1, 0))


def after(value, *others):
    return lax.optimization_barrier((value,) + others)[0]


def swap(block, axis):
    return lax.ppermute(block, axis, SWAP)


def dp_sum(block):
    if lax.axis_size("dp") == 2:
        return block.astype(F32) + swap(block, "dp").astype(F32)
    return lax.psum(block, "dp").astype(F32)


def line_route(lines, step):
    return [(i, (i + step) % lines) for i in range(lines)]


def along_line(block, lines):
    return [block] + [
        lax.ppermute(block, "l", line_route(lines, step)) for step in range(1, lines)
    ]


def per_device(axes, proj, short_filter, long_filter, w_out, dout, lengths, counts):
    rows, width = proj.shape[1], proj.shape[2] // 3
    chans, seq_len = long_filter.shape
    features = w_out.shape[1]
    batch = lengths.shape[0]
    ctx_size = seq_len // rows
    lines = lax.axis_size("l")
    split = Split(batch, lines, chans, axes[0] == "l")
    grad_scale = 1.0 / math.sqrt(batch * seq_len)
    assert batch == lax.axis_size("dp") and rows == LANES
    place = lax.axis_index(axes + ("dp",)).astype(jnp.int32).reshape(1)
    scalars = jnp.concatenate([place, lengths, counts])

    route = [(i, i + 1) for i in range(ctx_size - 1)]
    earlier = lax.ppermute(proj[0, rows - 2 :], axes, route)


    flat = (width, rows)
    width_of = features // CHUNKS
    parts = [
        along_line(after(w_out[:, i * width_of : (i + 1) * width_of], earlier), lines)
        for i in range(CHUNKS)
    ]
    inputs = (scalars, proj[0], earlier, short_filter)
    gated_t, query_t = call(
        functools.partial(prep_kernel, width=width, split=split),
        [(flat, BF16), (flat, F32)],
        inputs,
        1,
        far=(1, 3),
        scratch=[
            pltpu.VMEM((rows, 3 * width), BF16),
            pltpu.VMEM(short_filter.shape, F32),
            pltpu.SemaphoreType.DMA((2,)),
        ],
        flops=1 << 20,
    )

    (cot,) = call(
        functools.partial(cotangent_kernel, split=split),
        [((rows, features), BF16)],
        (scalars, after(dout[0], gated_t)),
        1,
        flops=1 << 20,
    )

    def exchange(block):
        return lax.all_to_all(block, axes, 0, 0, tiled=True)

    blocked = (ctx_size, chans, rows)
    tables = fft_tables(ctx_size)
    spec_shape = ((ctx_size + 1) * chans, 2 * LANES)
    sizes = {"blocks": ctx_size, "chans": chans}
    work = pltpu.VMEM(spec_shape, F32)
    signal = pltpu.VMEM(blocked, F32)
    fft_flops = 6 * spec_shape[0] * 2 * LANES * 2 * LANES
    (filt_spec,) = call(
        functools.partial(filter_kernel, **sizes),
        [(spec_shape, F32)],
        (after(long_filter, gated_t), *tables),
        scratch=[work],
        flops=fft_flops,
    )
    near = [
        jnp.concatenate(part[:1] + [after(p, filt_spec) for p in part[1:]]) for part in parts
    ]
    over = [swap(part, "h") for part in near]
    long_cols, gated_spec = call(
        functools.partial(forward_kernel, **sizes),
        [(blocked, BF16), (spec_shape, F32)],
        (exchange(gated_t.reshape(blocked)), filt_spec, *tables),
        scratch=[work, signal],
        flops=30 << 30,
    )
    long_t = exchange(long_cols).reshape(flat)
    over = [after(part, long_t) for part in over]
    weights = near + over + [swap(part, "c") for part in near + over]

    d_product_t, d_long_t = call(
        functools.partial(d_long_kernel, split=split),
        [(flat, F32), (flat, BF16)],
        (scalars, cot, query_t, *weights),
        1,
        flops=2 * rows * width * features,
    )
    d_long_cols = exchange(d_long_t.reshape(blocked))

    part = (lines * chans, width_of)
    product, *sums = call(
        functools.partial(partial_kernel, split=split, scale=grad_scale, tile=512),
        [((4, rows, lines * chans), BF16)] + [(part, BF16)] * (4 * CHUNKS),
        (scalars, long_t, query_t, after(cot, *weights)),
        1,
        scratch=[pltpu.VMEM(flat, F32)],
        flops=1024,
    )
    d_gated_cols, filter_part = call(
        functools.partial(backward_kernel, scale=grad_scale, **sizes),
        [(blocked, BF16), ((chans, seq_len), BF16)],
        (d_long_cols, filt_spec, gated_spec, *tables),
        scratch=[work, signal, work],
        flops=3 * fft_flops,
    )
    d_gated_t = exchange(d_gated_cols).reshape(flat)
    d_filter = dp_sum(filter_part)

    d_wout = []
    for chunk in range(CHUNKS):
        near_sum, over_sum, near_send, over_send = sums[chunk::CHUNKS]
        over_core, near_core = swap(over_send, "c"), swap(near_send, "c")
        over_sum = over_sum.astype(F32) + over_core.astype(F32)
        got = swap(over_sum.astype(BF16), "h")
        total = [
            near_sum[at].astype(F32) + near_core[at].astype(F32) + got[at].astype(F32)
            for at in (slice(i * chans, (i + 1) * chans) for i in range(lines))
        ]
        total_here = total[0]
        for step in range(1, lines):
            sent = total[lines - step].astype(BF16)
            total_here += lax.ppermute(sent, "l", line_route(lines, step)).astype(F32)
        d_wout.append(dp_sum(total_here.astype(BF16)))
    d_wout = jnp.concatenate(d_wout, axis=1)

    (output,) = call(
        functools.partial(output_kernel, tile=512),
        [((rows, features), BF16)],
        (product, *weights),
        flops=2 * rows * width * features,
    )

    (head,) = call(
        functools.partial(head_kernel, width=width, split=split),
        [((8, 3 * width), F32)],
        inputs + (d_product_t, long_t, d_gated_t),
        1,
        flops=1 << 20,
    )
    later = lax.ppermute(head[:2], axes, [(j, i) for i, j in route])
    (d_proj,) = call(
        functools.partial(proj_grad_kernel, width=width, split=split),
        [((rows, 3 * width), BF16)],
        inputs + (d_product_t, long_t, d_gated_t, later),
        1,
        flops=1 << 20,
    )
    return output[None], d_proj[None], d_wout, d_filter


def solution(mesh):
    ctx, dp = mesh.shape["ctx"], mesh.shape["dp"]
    if ctx == 16:
        axes, dims = ("l", "h", "c"), (4, 2, 2)
    else:
        axes, dims = ("h", "l", "c"), (2, ctx // 4, 2)
    fine = Mesh(mesh.devices.reshape(dims + (dp,)), axes + ("dp",))
    placed = (
        P("dp", axes, None),
        P(),
        P(axes, None),
        P(axes, None),
        P("dp", axes, None),
        P(),
        P(),
    )
    return jax.shard_map(
        functools.partial(per_device, axes),
        mesh=fine,
        in_specs=placed,
        out_specs=(P("dp", axes, None), P("dp", axes, None), P(axes, None), P(axes, None)),
        check_vma=False,
    )
```

```python
import functools
import math
import typing

import jax
import jax.numpy as jnp
import ml_dtypes
import numpy as np
from jax import lax
from jax.experimental import pallas as pl
from jax.experimental.pallas import tpu as pltpu
from jax.sharding import Mesh
from jax.sharding import PartitionSpec as P

F32 = jnp.float32
BF16 = jnp.bfloat16
LANES = 128
VMEM_LIMIT = 8 << 20
SMEM = pl.BlockSpec(memory_space=pltpu.SMEM)
HBM = pl.BlockSpec(memory_space=pltpu.HBM)


def split_bf16(values):
    high = values.astype(ml_dtypes.bfloat16)
    low = (values - high.astype(np.float64)).astype(ml_dtypes.bfloat16)
    return high, low


def fft_tables(blocks):
    size = 2 * blocks * LANES
    k1 = np.arange(blocks + 1)[:, None]
    lane = np.arange(LANES)
    angle = -2.0 * np.pi * (k1 * lane[None, :] % size) / size
    twist = np.stack([np.cos(angle), np.sin(angle)]).astype(np.float32)
    inner = -2.0 * np.pi * (lane[:, None] * lane[None, :] % LANES) / LANES
    cos, sin = np.cos(inner), np.sin(inner)
    matrix = np.block([[cos, sin], [-sin, cos]])
    high, low = split_bf16(matrix)
    return jnp.asarray(twist), jnp.asarray(np.stack([high, low]))


def real_fft(values):
    half = len(values)
    if half == 1:
        return [(values[0], None), (values[0], None)]
    even, odd = real_fft(values[0::2]), real_fft(values[1::2])
    out = [None] * (half + 1)
    out[0] = (even[0][0] + odd[0][0], None)
    out[half] = (even[0][0] - odd[0][0], None)
    out[half // 2] = (even[half // 2][0], -odd[half // 2][0])
    for k in range(1, half // 2):
        cos, sin = math.cos(math.pi * k / half), -math.sin(math.pi * k / half)
        (e_re, e_im), (o_re, o_im) = even[k], odd[k]
        t_re = o_re * cos - o_im * sin
        t_im = o_re * sin + o_im * cos
        out[k] = (e_re + t_re, e_im + t_im)
        out[half - k] = (e_re - t_re, t_im - e_im)
    return out


def real_ifft(spectrum):
    half = len(spectrum) - 1
    if half == 1:
        return [spectrum[0][0] + spectrum[1][0]]
    even = [None] * (half // 2 + 1)
    odd = [None] * (half // 2 + 1)
    even[0] = (spectrum[0][0] + spectrum[half][0], None)
    odd[0] = (spectrum[0][0] - spectrum[half][0], None)
    even[half // 2] = (2.0 * spectrum[half // 2][0], None)
    odd[half // 2] = (-2.0 * spectrum[half // 2][1], None)
    for k in range(1, half // 2):
        cos, sin = math.cos(math.pi * k / half), math.sin(math.pi * k / half)
        (a_re, a_im), (b_re, b_im) = spectrum[k], spectrum[half - k]
        even[k] = (a_re + b_re, a_im - b_im)
        d_re, d_im = a_re - b_re, a_im + b_im
        odd[k] = (d_re * cos - d_im * sin, d_re * sin + d_im * cos)
    out = [None] * half
    out[0::2] = real_ifft(even)
    out[1::2] = real_ifft(odd)
    return out


def split_dot(left, high, low, transposed):
    dims = (((1,), (1 if transposed else 0,)), ((), ()))
    dot = functools.partial(lax.dot_general, dimension_numbers=dims, preferred_element_type=F32)
    left_high = left.astype(BF16)
    left_low = (left - left_high.astype(F32)).astype(BF16)
    return dot(left_high, high) + (dot(left_low, high) + dot(left_high, low))


def to_spectrum(load, blocks, chans, twist, matrix, work):
    for first in range(0, chans, 8):
        rows = slice(first, first + 8)
        freqs = real_fft([load(n1, rows) for n1 in range(blocks)])
        for k1, (re, im) in enumerate(freqs):
            at = slice(k1 * chans + first, k1 * chans + first + 8)
            if k1 == 0:
                work[at, :LANES] = re
                work[at, LANES:] = jnp.zeros_like(re)
                continue
            cos, sin = twist[0, k1 : k1 + 1, :], twist[1, k1 : k1 + 1, :]
            if im is None:
                work[at, :LANES] = re * cos
                work[at, LANES:] = re * sin
            else:
                work[at, :LANES] = re * cos - im * sin
                work[at, LANES:] = re * sin + im * cos
    return split_dot(work[...], matrix[0], matrix[1], False)


def from_spectrum(spectrum, blocks, chans, twist, matrix, work, store):
    scale = 1.0 / (2 * blocks * LANES)
    work[...] = split_dot(spectrum, matrix[0], matrix[1], True)
    for first in range(0, chans, 8):
        rows = slice(first, first + 8)
        freqs = []
        for k1 in range(blocks + 1):
            at = slice(k1 * chans + first, k1 * chans + first + 8)
            re, im = work[at, :LANES] * scale, work[at, LANES:] * scale
            cos, sin = twist[0, k1 : k1 + 1, :], twist[1, k1 : k1 + 1, :]
            if k1 == 0:
                freqs.append((re, None))
            elif k1 == blocks:
                freqs.append((re * cos + im * sin, None))
            else:
                freqs.append((re * cos + im * sin, im * cos - re * sin))
        for n1, value in enumerate(real_ifft(freqs)):
            store(n1, rows, value)


def times(a, b):
    a_re, a_im, b_re, b_im = a[:, :LANES], a[:, LANES:], b[:, :LANES], b[:, LANES:]
    return jnp.concatenate([a_re * b_re - a_im * b_im, a_re * b_im + a_im * b_re], axis=1)


def conj_times(a, b):
    a_re, a_im, b_re, b_im = a[:, :LANES], a[:, LANES:], b[:, :LANES], b[:, LANES:]
    return jnp.concatenate([a_re * b_re + a_im * b_im, a_re * b_im - a_im * b_re], axis=1)


def filter_kernel(filt, twist, matrix, spec, work, *, blocks, chans):
    def load(n1, rows):
        return filt[rows, n1 * LANES : (n1 + 1) * LANES]

    spec[...] = to_spectrum(load, blocks, chans, twist, matrix, work)


def forward_kernel(
    gated, filt_spec, twist, matrix, long_out, gated_spec, work, signal, *, blocks, chans
):
    for n1 in range(blocks):
        signal[n1] = gated[n1].astype(F32)

    def load(n1, rows):
        return signal[n1, rows, :]

    spec = to_spectrum(load, blocks, chans, twist, matrix, work)
    gated_spec[...] = spec

    def store(n1, rows, value):
        signal[n1, rows, :] = value

    from_spectrum(times(spec, filt_spec[...]), blocks, chans, twist, matrix, work, store)
    for n1 in range(blocks):
        long_out[n1] = signal[n1].astype(BF16)


def backward_kernel(
    d_long,
    filt_spec,
    gated_spec,
    twist,
    matrix,
    d_gated,
    d_filter,
    work,
    signal,
    held,
    *,
    blocks,
    chans,
    scale,
):
    for n1 in range(blocks):
        signal[n1] = d_long[n1].astype(F32)

    def load(n1, rows):
        return signal[n1, rows, :]

    held[...] = to_spectrum(load, blocks, chans, twist, matrix, work)

    def store(n1, rows, value):
        signal[n1, rows, :] = value

    spec = conj_times(filt_spec[...], held[...])
    from_spectrum(spec, blocks, chans, twist, matrix, work, store)
    for n1 in range(blocks):
        d_gated[n1] = signal[n1].astype(BF16)
    spec = conj_times(gated_spec[...], held[...])
    from_spectrum(spec, blocks, chans, twist, matrix, work, store)
    for n1 in range(blocks):
        d_filter[:, n1 * LANES : (n1 + 1) * LANES] = (signal[n1] * scale).astype(BF16)


class Split(typing.NamedTuple):
    samples: int
    lines: int
    chans: int
    line_first: bool


def mixed_stream(stream, proj, earlier, taps, room, width):
    rows = proj.shape[0]
    row = lax.broadcasted_iota(jnp.int32, (rows, 1), 0)
    past_row = lax.broadcasted_iota(jnp.int32, (2, 1), 0)
    cols = slice(stream * width, (stream + 1) * width)
    masked = jnp.where(row < room, proj[:, cols].astype(F32), 0.0)
    past = jnp.where(past_row < room + 2, earlier[:, cols].astype(F32), 0.0)
    mixed = taps[0:1, cols] * masked
    for tap in range(1, 3):
        shifted = pltpu.roll(masked, tap, 0)
        for r in range(tap):
            shifted = jnp.where(row == r, past[2 - tap + r : 3 - tap + r, :], shifted)
        mixed = mixed + taps[tap : tap + 1, cols] * shifted
    return mixed


def prep_kernel(scalars, proj, earlier, taps, gated_t, query_t, *, width, split):
    room = room_left(scalars, split, proj.shape[0])
    query, key, value = (
        mixed_stream(stream, proj, earlier, taps, room, width) for stream in range(3)
    )
    gated_t[...] = (key * value).T.astype(BF16)
    query_t[...] = query.T


def room_left(scalars, split, rows):
    group, sample = scalars[0] // split.samples, scalars[0] % split.samples
    length = scalars[1]
    for other in range(1, split.samples):
        length = jnp.where(sample == other, scalars[1 + other], length)
    return length - group * rows


def loss_weight(scalars, split):
    sample = scalars[0] % split.samples
    total, mine = jnp.float32(0), jnp.float32(0)
    for other in range(split.samples):
        count = scalars[1 + split.samples + other].astype(F32)
        total = total + count
        mine = jnp.where(sample == other, count, mine)
    return jnp.full((1, LANES), mine * split.samples) / jnp.full((1, LANES), total)


def natural_row(scalars, rel_h, rel_c, step, split):
    group = scalars[0] // split.samples
    lines, chans = split.lines, split.chans
    c = (group % 2 + rel_c) % 2
    if split.line_first:
        h, line = group // 2 % 2, group // 4
    else:
        h, line = group // (2 * lines), group // 2 % lines
    h, line = (h + rel_h) % 2, (line + lines - step) % lines
    at = (line * 2 + h) * 2 + c if split.line_first else (h * lines + line) * 2 + c
    return pl.multiple_of(at * chans, chans)


PIECES = ((0, 0), (1, 0), (0, 1), (1, 1))
CHUNKS = 1


def cotangent_kernel(scalars, dout, cot, *, split):
    rows = dout.shape[0]
    row = lax.broadcasted_iota(jnp.int32, (rows, 1), 0)
    mask = jnp.where(row < room_left(scalars, split, rows), 1.0, 0.0)
    weight = loss_weight(scalars, split)[:, :1]
    cot[...] = (dout[...].astype(F32) * mask * weight).astype(BF16)


def d_long_kernel(scalars, cot, query_t, *refs, split):
    *weights, d_product_t, d_long_t = refs
    lines, chans = split.lines, split.chans
    part = cot.shape[1] // CHUNKS
    for piece, (rel_h, rel_c) in enumerate(PIECES):
        got = sum(
            lax.dot_general(
                weights[piece * CHUNKS + chunk][...],
                cot[:, chunk * part : (chunk + 1) * part],
                (((1,), (1,)), ((), ())),
                preferred_element_type=F32,
            )
            for chunk in range(CHUNKS)
        )
        for line in range(lines):
            at = natural_row(scalars, rel_h, rel_c, line, split)
            d_product_t[pl.ds(at, chans), :] = got[line * chans : (line + 1) * chans]
    d_long_t[...] = (d_product_t[...] * query_t[...]).astype(BF16)


def partial_kernel(
    scalars, long_t, query_t, cot, product, *refs, split, scale, tile
):
    *parts, product_t = refs
    lines, chans = split.lines, split.chans
    part = cot.shape[1] // CHUNKS
    product_t[...] = query_t[...] * long_t[...].astype(F32)
    for piece, (rel_h, rel_c) in enumerate(PIECES):
        left = jnp.concatenate(
            [
                product_t[pl.ds(natural_row(scalars, rel_h, rel_c, line, split), chans), :]
                for line in range(lines)
            ],
            axis=0,
        )
        product[piece] = left.T.astype(BF16)
        left = left.astype(BF16)
        for first in range(0, cot.shape[1], tile):
            cols = slice(first, first + tile)
            got = jnp.dot(left, cot[:, cols], preferred_element_type=F32) * scale
            out = parts[(2 * rel_c + rel_h) * CHUNKS + first // part]
            out[:, first % part : first % part + tile] = got.astype(BF16)


def output_kernel(product, *refs, tile):
    *weights, out = refs
    part = out.shape[1] // CHUNKS
    for first in range(0, out.shape[1], tile):
        chunk, cols = first // part, slice(first % part, first % part + tile)
        total = sum(
            jnp.dot(
                product[piece], weights[piece * CHUNKS + chunk][:, cols], preferred_element_type=F32
            )
            for piece in range(4)
        )
        out[:, first : first + tile] = total.astype(BF16)


def mixed_grads(d_product_t, long_t, d_gated_t, key, value, rows):
    d_query = (d_product_t[...] * long_t[...].astype(F32)).T[:rows]
    d_gated = d_gated_t[...].astype(F32).T[:rows]
    return d_query, d_gated * value[:rows], d_gated * key[:rows]


def head_kernel(
    scalars, proj, earlier, taps, d_product_t, long_t, d_gated_t, head, *, width, split
):
    room = room_left(scalars, split, proj.shape[0])
    key, value = (mixed_stream(i, proj, earlier, taps, room, width) for i in (1, 2))
    grads = mixed_grads(d_product_t, long_t, d_gated_t, key, value, 8)
    for stream, grad in enumerate(grads):
        head[:, stream * width : (stream + 1) * width] = grad


def proj_grad_kernel(
    scalars,
    proj,
    earlier,
    taps,
    d_product_t,
    long_t,
    d_gated_t,
    later,
    d_proj,
    *,
    width,
    split,
):
    rows = proj.shape[0]
    row = lax.broadcasted_iota(jnp.int32, (rows, 1), 0)
    room = room_left(scalars, split, rows)
    key, value = (mixed_stream(i, proj, earlier, taps, room, width) for i in (1, 2))
    grads = mixed_grads(d_product_t, long_t, d_gated_t, key, value, rows)
    for stream, grad in enumerate(grads):
        cols = slice(stream * width, (stream + 1) * width)
        total = taps[0:1, cols] * grad
        for tap in range(1, 3):
            shifted = pltpu.roll(grad, rows - tap, 0)
            for r in range(tap):
                shifted = jnp.where(row == rows - tap + r, later[r : r + 1, cols], shifted)
            total = total + taps[tap : tap + 1, cols] * shifted
        d_proj[:, cols] = jnp.where(row < room, total, 0.0).astype(BF16)


def call(kernel, outs, args, scalars=0, scratch=(), flops=0, far=()):
    def full(value):
        return pl.BlockSpec(value.shape, lambda i, n=len(value.shape): (0,) * n)

    out_shape = [jax.ShapeDtypeStruct(shape, dtype) for shape, dtype in outs]
    return pl.pallas_call(
        kernel,
        grid=(1,),
        out_shape=out_shape,
        in_specs=[
            SMEM if i < scalars else HBM if i in far else full(v) for i, v in enumerate(args)
        ],
        out_specs=[full(v) for v in out_shape],
        scratch_shapes=list(scratch),
        compiler_params=pltpu.CompilerParams(vmem_limit_bytes=VMEM_LIMIT),
        cost_estimate=pl.CostEstimate(flops=flops, bytes_accessed=1024, transcendentals=0),
    )(*args)


SWAP = ((0, 1), (1, 0))


def after(value, *others):
    return lax.optimization_barrier((value,) + others)[0]


def swap(block, axis):
    return lax.ppermute(block, axis, SWAP)


def dp_sum(block):
    if lax.axis_size("dp") == 2:
        return block.astype(F32) + swap(block, "dp").astype(F32)
    return lax.psum(block, "dp").astype(F32)


def line_route(lines, step):
    return [(i, (i + step) % lines) for i in range(lines)]


def along_line(block, lines):
    return [block] + [
        lax.ppermute(block, "l", line_route(lines, step)) for step in range(1, lines)
    ]


def per_device(axes, proj, short_filter, long_filter, w_out, dout, lengths, counts):
    rows, width = proj.shape[1], proj.shape[2] // 3
    chans, seq_len = long_filter.shape
    features = w_out.shape[1]
    batch = lengths.shape[0]
    ctx_size = seq_len // rows
    lines = lax.axis_size("l")
    split = Split(batch, lines, chans, axes[0] == "l")
    grad_scale = 1.0 / math.sqrt(batch * seq_len)
    assert batch == lax.axis_size("dp") and rows == LANES
    place = lax.axis_index(axes + ("dp",)).astype(jnp.int32).reshape(1)
    scalars = jnp.concatenate([place, lengths, counts])

    route = [(i, i + 1) for i in range(ctx_size - 1)]
    earlier = lax.ppermute(proj[0, rows - 2 :], axes, route)


    flat = (width, rows)
    width_of = features // CHUNKS
    parts = [
        along_line(after(w_out[:, i * width_of : (i + 1) * width_of], earlier), lines)
        for i in range(CHUNKS)
    ]
    inputs = (scalars, proj[0], earlier, short_filter)
    gated_t, query_t = call(
        functools.partial(prep_kernel, width=width, split=split),
        [(flat, BF16), (flat, F32)],
        inputs,
        1,
        flops=1 << 20,
    )

    (cot,) = call(
        functools.partial(cotangent_kernel, split=split),
        [((rows, features), BF16)],
        (scalars, after(dout[0], gated_t)),
        1,
        flops=1 << 20,
    )

    def exchange(block):
        return lax.all_to_all(block, axes, 0, 0, tiled=True)

    blocked = (ctx_size, chans, rows)
    tables = fft_tables(ctx_size)
    spec_shape = ((ctx_size + 1) * chans, 2 * LANES)
    sizes = {"blocks": ctx_size, "chans": chans}
    work = pltpu.VMEM(spec_shape, F32)
    signal = pltpu.VMEM(blocked, F32)
    fft_flops = 6 * spec_shape[0] * 2 * LANES * 2 * LANES
    (filt_spec,) = call(
        functools.partial(filter_kernel, **sizes),
        [(spec_shape, F32)],
        (after(long_filter, gated_t), *tables),
        scratch=[work],
        flops=fft_flops,
    )
    near = [
        jnp.concatenate(part[:1] + [after(p, filt_spec) for p in part[1:]]) for part in parts
    ]
    over = [swap(part, "h") for part in near]
    long_cols, gated_spec = call(
        functools.partial(forward_kernel, **sizes),
        [(blocked, BF16), (spec_shape, F32)],
        (exchange(gated_t.reshape(blocked)), filt_spec, *tables),
        scratch=[work, signal],
        flops=30 << 30,
    )
    long_t = exchange(long_cols).reshape(flat)
    over = [after(part, long_t) for part in over]
    weights = near + over + [swap(part, "c") for part in near + over]

    d_product_t, d_long_t = call(
        functools.partial(d_long_kernel, split=split),
        [(flat, F32), (flat, BF16)],
        (scalars, cot, query_t, *weights),
        1,
        flops=2 * rows * width * features,
    )
    d_long_cols = exchange(d_long_t.reshape(blocked))

    part = (lines * chans, width_of)
    product, *sums = call(
        functools.partial(partial_kernel, split=split, scale=grad_scale, tile=512),
        [((4, rows, lines * chans), BF16)] + [(part, BF16)] * (4 * CHUNKS),
        (scalars, long_t, query_t, after(cot, d_long_t)),
        1,
        scratch=[pltpu.VMEM(flat, F32)],
        flops=1024,
    )
    d_gated_cols, filter_part = call(
        functools.partial(backward_kernel, scale=grad_scale, **sizes),
        [(blocked, BF16), ((chans, seq_len), BF16)],
        (d_long_cols, filt_spec, gated_spec, *tables),
        scratch=[work, signal, work],
        flops=3 * fft_flops,
    )
    (output,) = call(
        functools.partial(output_kernel, tile=512),
        [((rows, features), BF16)],
        (product, *weights),
        flops=2 * rows * width * features,
    )

    near_sum, over_sum, near_send, over_send = sums
    over_core, near_core = swap(over_send, "c"), swap(near_send, "c")
    over_sum = over_sum.astype(F32) + after(over_core, output).astype(F32)
    got = after(swap(over_sum.astype(BF16), "h"), filter_part)
    total = [
        near_sum[at].astype(F32) + near_core[at].astype(F32) + got[at].astype(F32)
        for at in (slice(i * chans, (i + 1) * chans) for i in range(lines))
    ]
    sent = [total[lines - step].astype(BF16) for step in range(1, lines)]
    d_filter = dp_sum(filter_part)
    total_here = total[0]
    for step, block in enumerate(sent, 1):
        got = after(lax.ppermute(block, "l", line_route(lines, step)), d_filter)
        total_here += got.astype(F32)
    d_wout = dp_sum(total_here.astype(BF16))

    d_gated_t = exchange(after(d_gated_cols, *sent)).reshape(flat)

    (head,) = call(
        functools.partial(head_kernel, width=width, split=split),
        [((8, 3 * width), F32)],
        inputs + (d_product_t, long_t, d_gated_t),
        1,
        flops=1 << 20,
    )
    later = lax.ppermute(head[:2], axes, [(j, i) for i, j in route])
    (d_proj,) = call(
        functools.partial(proj_grad_kernel, width=width, split=split),
        [((rows, 3 * width), BF16)],
        inputs + (d_product_t, long_t, d_gated_t, later),
        1,
        flops=1 << 20,
    )
    return output[None], d_proj[None], d_wout, d_filter


def solution(mesh):
    ctx, dp = mesh.shape["ctx"], mesh.shape["dp"]
    if ctx == 16:
        axes, dims = ("l", "h", "c"), (4, 2, 2)
    else:
        axes, dims = ("h", "l", "c"), (2, ctx // 4, 2)
    fine = Mesh(mesh.devices.reshape(dims + (dp,)), axes + ("dp",))
    placed = (
        P("dp", axes, None),
        P(),
        P(axes, None),
        P(axes, None),
        P("dp", axes, None),
        P(),
        P(),
    )
    return jax.shard_map(
        functools.partial(per_device, axes),
        mesh=fine,
        in_specs=placed,
        out_specs=(P("dp", axes, None), P("dp", axes, None), P(axes, None), P(axes, None)),
        check_vma=False,
    )
```

```python
import functools
import math
import typing

import jax
import jax.numpy as jnp
import ml_dtypes
import numpy as np
from jax import lax
from jax.experimental import pallas as pl
from jax.experimental.pallas import tpu as pltpu
from jax.sharding import Mesh
from jax.sharding import PartitionSpec as P

F32 = jnp.float32
BF16 = jnp.bfloat16
LANES = 128
VMEM_LIMIT = 8 << 20
SMEM = pl.BlockSpec(memory_space=pltpu.SMEM)
HBM = pl.BlockSpec(memory_space=pltpu.HBM)


def split_bf16(values):
    high = values.astype(ml_dtypes.bfloat16)
    low = (values - high.astype(np.float64)).astype(ml_dtypes.bfloat16)
    return high, low


def fft_tables(blocks):
    size = 2 * blocks * LANES
    k1 = np.arange(blocks + 1)[:, None]
    lane = np.arange(LANES)
    angle = -2.0 * np.pi * (k1 * lane[None, :] % size) / size
    twist = np.stack([np.cos(angle), np.sin(angle)]).astype(np.float32)
    inner = -2.0 * np.pi * (lane[:, None] * lane[None, :] % LANES) / LANES
    cos, sin = np.cos(inner), np.sin(inner)
    matrix = np.block([[cos, sin], [-sin, cos]])
    high, low = split_bf16(matrix)
    return jnp.asarray(twist), jnp.asarray(np.stack([high, low]))


def real_fft(values):
    half = len(values)
    if half == 1:
        return [(values[0], None), (values[0], None)]
    even, odd = real_fft(values[0::2]), real_fft(values[1::2])
    out = [None] * (half + 1)
    out[0] = (even[0][0] + odd[0][0], None)
    out[half] = (even[0][0] - odd[0][0], None)
    out[half // 2] = (even[half // 2][0], -odd[half // 2][0])
    for k in range(1, half // 2):
        cos, sin = math.cos(math.pi * k / half), -math.sin(math.pi * k / half)
        (e_re, e_im), (o_re, o_im) = even[k], odd[k]
        t_re = o_re * cos - o_im * sin
        t_im = o_re * sin + o_im * cos
        out[k] = (e_re + t_re, e_im + t_im)
        out[half - k] = (e_re - t_re, t_im - e_im)
    return out


def real_ifft(spectrum):
    half = len(spectrum) - 1
    if half == 1:
        return [spectrum[0][0] + spectrum[1][0]]
    even = [None] * (half // 2 + 1)
    odd = [None] * (half // 2 + 1)
    even[0] = (spectrum[0][0] + spectrum[half][0], None)
    odd[0] = (spectrum[0][0] - spectrum[half][0], None)
    even[half // 2] = (2.0 * spectrum[half // 2][0], None)
    odd[half // 2] = (-2.0 * spectrum[half // 2][1], None)
    for k in range(1, half // 2):
        cos, sin = math.cos(math.pi * k / half), math.sin(math.pi * k / half)
        (a_re, a_im), (b_re, b_im) = spectrum[k], spectrum[half - k]
        even[k] = (a_re + b_re, a_im - b_im)
        d_re, d_im = a_re - b_re, a_im + b_im
        odd[k] = (d_re * cos - d_im * sin, d_re * sin + d_im * cos)
    out = [None] * half
    out[0::2] = real_ifft(even)
    out[1::2] = real_ifft(odd)
    return out


def split_dot(left, high, low, transposed):
    dims = (((1,), (1 if transposed else 0,)), ((), ()))
    dot = functools.partial(lax.dot_general, dimension_numbers=dims, preferred_element_type=F32)
    left_high = left.astype(BF16)
    left_low = (left - left_high.astype(F32)).astype(BF16)
    return dot(left_high, high) + (dot(left_low, high) + dot(left_high, low))


def to_spectrum(load, blocks, chans, twist, matrix, work):
    for first in range(0, chans, 8):
        rows = slice(first, first + 8)
        freqs = real_fft([load(n1, rows) for n1 in range(blocks)])
        for k1, (re, im) in enumerate(freqs):
            at = slice(k1 * chans + first, k1 * chans + first + 8)
            if k1 == 0:
                work[at, :LANES] = re
                work[at, LANES:] = jnp.zeros_like(re)
                continue
            cos, sin = twist[0, k1 : k1 + 1, :], twist[1, k1 : k1 + 1, :]
            if im is None:
                work[at, :LANES] = re * cos
                work[at, LANES:] = re * sin
            else:
                work[at, :LANES] = re * cos - im * sin
                work[at, LANES:] = re * sin + im * cos
    return split_dot(work[...], matrix[0], matrix[1], False)


def from_spectrum(spectrum, blocks, chans, twist, matrix, work, store):
    scale = 1.0 / (2 * blocks * LANES)
    work[...] = split_dot(spectrum, matrix[0], matrix[1], True)
    for first in range(0, chans, 8):
        rows = slice(first, first + 8)
        freqs = []
        for k1 in range(blocks + 1):
            at = slice(k1 * chans + first, k1 * chans + first + 8)
            re, im = work[at, :LANES] * scale, work[at, LANES:] * scale
            cos, sin = twist[0, k1 : k1 + 1, :], twist[1, k1 : k1 + 1, :]
            if k1 == 0:
                freqs.append((re, None))
            elif k1 == blocks:
                freqs.append((re * cos + im * sin, None))
            else:
                freqs.append((re * cos + im * sin, im * cos - re * sin))
        for n1, value in enumerate(real_ifft(freqs)):
            store(n1, rows, value)


def times(a, b):
    a_re, a_im, b_re, b_im = a[:, :LANES], a[:, LANES:], b[:, :LANES], b[:, LANES:]
    return jnp.concatenate([a_re * b_re - a_im * b_im, a_re * b_im + a_im * b_re], axis=1)


def conj_times(a, b):
    a_re, a_im, b_re, b_im = a[:, :LANES], a[:, LANES:], b[:, :LANES], b[:, LANES:]
    return jnp.concatenate([a_re * b_re + a_im * b_im, a_re * b_im - a_im * b_re], axis=1)


def filter_kernel(filt, twist, matrix, spec, work, *, blocks, chans):
    def load(n1, rows):
        return filt[rows, n1 * LANES : (n1 + 1) * LANES]

    spec[...] = to_spectrum(load, blocks, chans, twist, matrix, work)


def forward_kernel(
    gated, filt_spec, twist, matrix, long_out, work, signal, *, blocks, chans
):
    for n1 in range(blocks):
        signal[n1] = gated[n1].astype(F32)

    def load(n1, rows):
        return signal[n1, rows, :]

    spec = to_spectrum(load, blocks, chans, twist, matrix, work)

    def store(n1, rows, value):
        signal[n1, rows, :] = value

    from_spectrum(times(spec, filt_spec[...]), blocks, chans, twist, matrix, work, store)
    for n1 in range(blocks):
        long_out[n1] = signal[n1].astype(BF16)


def backward_kernel(
    d_long,
    filt_spec,
    gated,
    twist,
    matrix,
    d_gated,
    d_filter,
    work,
    signal,
    held,
    *,
    blocks,
    chans,
    scale,
):
    for n1 in range(blocks):
        signal[n1] = d_long[n1].astype(F32)

    def load(n1, rows):
        return signal[n1, rows, :]

    held[...] = to_spectrum(load, blocks, chans, twist, matrix, work)

    def store(n1, rows, value):
        signal[n1, rows, :] = value

    spec = conj_times(filt_spec[...], held[...])
    from_spectrum(spec, blocks, chans, twist, matrix, work, store)
    for n1 in range(blocks):
        d_gated[n1] = signal[n1].astype(BF16)
    for n1 in range(blocks):
        signal[n1] = gated[n1].astype(F32)
    spec = conj_times(to_spectrum(load, blocks, chans, twist, matrix, work), held[...])
    from_spectrum(spec, blocks, chans, twist, matrix, work, store)
    for n1 in range(blocks):
        d_filter[:, n1 * LANES : (n1 + 1) * LANES] = (signal[n1] * scale).astype(BF16)


class Split(typing.NamedTuple):
    samples: int
    lines: int
    chans: int
    line_first: bool


def mixed_stream(stream, proj, earlier, taps, room, width):
    rows = proj.shape[0]
    row = lax.broadcasted_iota(jnp.int32, (rows, 1), 0)
    past_row = lax.broadcasted_iota(jnp.int32, (2, 1), 0)
    cols = slice(stream * width, (stream + 1) * width)
    masked = jnp.where(row < room, proj[:, cols].astype(F32), 0.0)
    past = jnp.where(past_row < room + 2, earlier[:, cols].astype(F32), 0.0)
    mixed = taps[0:1, cols] * masked
    for tap in range(1, 3):
        shifted = pltpu.roll(masked, tap, 0)
        for r in range(tap):
            shifted = jnp.where(row == r, past[2 - tap + r : 3 - tap + r, :], shifted)
        mixed = mixed + taps[tap : tap + 1, cols] * shifted
    return mixed


def prep_kernel(scalars, proj, earlier, taps, gated_t, query_t, *, width, split):
    room = room_left(scalars, split, proj.shape[0])
    query, key, value = (
        mixed_stream(stream, proj, earlier, taps, room, width) for stream in range(3)
    )
    gated_t[...] = (key * value).T.astype(BF16)
    query_t[...] = query.T


def room_left(scalars, split, rows):
    group, sample = scalars[0] // split.samples, scalars[0] % split.samples
    length = scalars[1]
    for other in range(1, split.samples):
        length = jnp.where(sample == other, scalars[1 + other], length)
    return length - group * rows


def loss_weight(scalars, split):
    sample = scalars[0] % split.samples
    total, mine = jnp.float32(0), jnp.float32(0)
    for other in range(split.samples):
        count = scalars[1 + split.samples + other].astype(F32)
        total = total + count
        mine = jnp.where(sample == other, count, mine)
    return jnp.full((1, LANES), mine * split.samples) / jnp.full((1, LANES), total)


def natural_row(scalars, rel_h, rel_c, step, split):
    group = scalars[0] // split.samples
    lines, chans = split.lines, split.chans
    c = (group % 2 + rel_c) % 2
    if split.line_first:
        h, line = group // 2 % 2, group // 4
    else:
        h, line = group // (2 * lines), group // 2 % lines
    h, line = (h + rel_h) % 2, (line + lines - step) % lines
    at = (line * 2 + h) * 2 + c if split.line_first else (h * lines + line) * 2 + c
    return pl.multiple_of(at * chans, chans)


PIECES = ((0, 0), (1, 0), (0, 1), (1, 1))
CHUNKS = 1


def cotangent_kernel(scalars, dout, cot, *, split):
    rows = dout.shape[0]
    row = lax.broadcasted_iota(jnp.int32, (rows, 1), 0)
    mask = jnp.where(row < room_left(scalars, split, rows), 1.0, 0.0)
    weight = loss_weight(scalars, split)[:, :1]
    cot[...] = (dout[...].astype(F32) * mask * weight).astype(BF16)


def d_long_kernel(scalars, cot, query_t, *refs, split):
    *weights, d_product_t, d_long_t = refs
    lines, chans = split.lines, split.chans
    part = cot.shape[1] // CHUNKS
    for piece, (rel_h, rel_c) in enumerate(PIECES):
        got = sum(
            lax.dot_general(
                weights[piece * CHUNKS + chunk][...],
                cot[:, chunk * part : (chunk + 1) * part],
                (((1,), (1,)), ((), ())),
                preferred_element_type=F32,
            )
            for chunk in range(CHUNKS)
        )
        for line in range(lines):
            at = natural_row(scalars, rel_h, rel_c, line, split)
            d_product_t[pl.ds(at, chans), :] = got[line * chans : (line + 1) * chans]
    d_long_t[...] = (d_product_t[...] * query_t[...]).astype(BF16)


def partial_kernel(
    scalars, long_t, query_t, cot, product, *refs, split, scale, tile
):
    *parts, product_t = refs
    lines, chans = split.lines, split.chans
    part = cot.shape[1] // CHUNKS
    product_t[...] = query_t[...] * long_t[...].astype(F32)
    for piece, (rel_h, rel_c) in enumerate(PIECES):
        left = jnp.concatenate(
            [
                product_t[pl.ds(natural_row(scalars, rel_h, rel_c, line, split), chans), :]
                for line in range(lines)
            ],
            axis=0,
        )
        product[piece] = left.T.astype(BF16)
        left = left.astype(BF16)
        for first in range(0, cot.shape[1], tile):
            cols = slice(first, first + tile)
            got = jnp.dot(left, cot[:, cols], preferred_element_type=F32) * scale
            out = parts[(2 * rel_c + rel_h) * CHUNKS + first // part]
            out[:, first % part : first % part + tile] = got.astype(BF16)


def output_kernel(product, *refs, tile):
    *weights, out = refs
    part = out.shape[1] // CHUNKS
    for first in range(0, out.shape[1], tile):
        chunk, cols = first // part, slice(first % part, first % part + tile)
        total = sum(
            jnp.dot(
                product[piece], weights[piece * CHUNKS + chunk][:, cols], preferred_element_type=F32
            )
            for piece in range(4)
        )
        out[:, first : first + tile] = total.astype(BF16)


def mixed_grads(d_product_t, long_t, d_gated_t, key, value, rows):
    d_query = (d_product_t[...] * long_t[...].astype(F32)).T[:rows]
    d_gated = d_gated_t[...].astype(F32).T[:rows]
    return d_query, d_gated * value[:rows], d_gated * key[:rows]


def head_kernel(
    scalars, proj, earlier, taps, d_product_t, long_t, d_gated_t, head, *, width, split
):
    room = room_left(scalars, split, proj.shape[0])
    key, value = (mixed_stream(i, proj, earlier, taps, room, width) for i in (1, 2))
    grads = mixed_grads(d_product_t, long_t, d_gated_t, key, value, 8)
    for stream, grad in enumerate(grads):
        head[:, stream * width : (stream + 1) * width] = grad


def proj_grad_kernel(
    scalars,
    proj,
    earlier,
    taps,
    d_product_t,
    long_t,
    d_gated_t,
    later,
    d_proj,
    *,
    width,
    split,
):
    rows = proj.shape[0]
    row = lax.broadcasted_iota(jnp.int32, (rows, 1), 0)
    room = room_left(scalars, split, rows)
    key, value = (mixed_stream(i, proj, earlier, taps, room, width) for i in (1, 2))
    grads = mixed_grads(d_product_t, long_t, d_gated_t, key, value, rows)
    for stream, grad in enumerate(grads):
        cols = slice(stream * width, (stream + 1) * width)
        total = taps[0:1, cols] * grad
        for tap in range(1, 3):
            shifted = pltpu.roll(grad, rows - tap, 0)
            for r in range(tap):
                shifted = jnp.where(row == rows - tap + r, later[r : r + 1, cols], shifted)
            total = total + taps[tap : tap + 1, cols] * shifted
        d_proj[:, cols] = jnp.where(row < room, total, 0.0).astype(BF16)


def call(kernel, outs, args, scalars=0, scratch=(), flops=0, far=()):
    def full(value):
        return pl.BlockSpec(value.shape, lambda i, n=len(value.shape): (0,) * n)

    out_shape = [jax.ShapeDtypeStruct(shape, dtype) for shape, dtype in outs]
    return pl.pallas_call(
        kernel,
        grid=(1,),
        out_shape=out_shape,
        in_specs=[
            SMEM if i < scalars else HBM if i in far else full(v) for i, v in enumerate(args)
        ],
        out_specs=[full(v) for v in out_shape],
        scratch_shapes=list(scratch),
        compiler_params=pltpu.CompilerParams(vmem_limit_bytes=VMEM_LIMIT),
        cost_estimate=pl.CostEstimate(flops=flops, bytes_accessed=1024, transcendentals=0),
    )(*args)


SWAP = ((0, 1), (1, 0))


def after(value, *others):
    return lax.optimization_barrier((value,) + others)[0]


def swap(block, axis):
    return lax.ppermute(block, axis, SWAP)


def dp_start(block):
    return swap(block, "dp") if lax.axis_size("dp") == 2 else lax.psum(block, "dp")


def dp_finish(block, got):
    if lax.axis_size("dp") == 2:
        return block.astype(F32) + got.astype(F32)
    return got.astype(F32)


def line_route(lines, step):
    return [(i, (i + step) % lines) for i in range(lines)]


def along_line(block, lines):
    return [block] + [
        lax.ppermute(block, "l", line_route(lines, step)) for step in range(1, lines)
    ]


def per_device(axes, proj, short_filter, long_filter, w_out, dout, lengths, counts):
    rows, width = proj.shape[1], proj.shape[2] // 3
    chans, seq_len = long_filter.shape
    features = w_out.shape[1]
    batch = lengths.shape[0]
    ctx_size = seq_len // rows
    lines = lax.axis_size("l")
    split = Split(batch, lines, chans, axes[0] == "l")
    grad_scale = 1.0 / math.sqrt(batch * seq_len)
    assert batch == lax.axis_size("dp") and rows == LANES
    place = lax.axis_index(axes + ("dp",)).astype(jnp.int32).reshape(1)
    scalars = jnp.concatenate([place, lengths, counts])

    route = [(i, i + 1) for i in range(ctx_size - 1)]
    tail = proj[0, rows - 2 :]
    earlier = lax.ppermute(tail, axes, route)


    flat = (width, rows)
    width_of = features // CHUNKS
    parts = [
        along_line(after(w_out[:, i * width_of : (i + 1) * width_of], tail), lines)
        for i in range(CHUNKS)
    ]
    inputs = (scalars, proj[0], earlier, short_filter)
    gated_t, query_t = call(
        functools.partial(prep_kernel, width=width, split=split),
        [(flat, BF16), (flat, F32)],
        inputs,
        1,
        flops=1 << 20,
    )

    (cot,) = call(
        functools.partial(cotangent_kernel, split=split),
        [((rows, features), BF16)],
        (scalars, after(dout[0], gated_t)),
        1,
        flops=1 << 20,
    )

    def exchange(block):
        return lax.all_to_all(block, axes, 0, 0, tiled=True)

    blocked = (ctx_size, chans, rows)
    tables = fft_tables(ctx_size)
    spec_shape = ((ctx_size + 1) * chans, 2 * LANES)
    sizes = {"blocks": ctx_size, "chans": chans}
    work = pltpu.VMEM(spec_shape, F32)
    signal = pltpu.VMEM(blocked, F32)
    fft_flops = 6 * spec_shape[0] * 2 * LANES * 2 * LANES
    (filt_spec,) = call(
        functools.partial(filter_kernel, **sizes),
        [(spec_shape, F32)],
        (after(long_filter, gated_t), *tables),
        scratch=[work],
        flops=fft_flops,
    )
    near = [
        jnp.concatenate([after(part[0], filt_spec)] + part[1:]) for part in parts
    ]
    over = [swap(part, "h") for part in near]
    gated_cols = exchange(gated_t.reshape(blocked))
    (long_cols,) = call(
        functools.partial(forward_kernel, **sizes),
        [(blocked, BF16)],
        (gated_cols, filt_spec, *tables),
        scratch=[work, signal],
        flops=30 << 30,
    )
    long_t = exchange(long_cols).reshape(flat)
    over = [after(part, long_t) for part in over]
    weights = near + over + [swap(part, "c") for part in near + over]

    d_product_t, d_long_t = call(
        functools.partial(d_long_kernel, split=split),
        [(flat, F32), (flat, BF16)],
        (scalars, cot, query_t, *weights),
        1,
        flops=2 * rows * width * features,
    )
    d_long_cols = exchange(d_long_t.reshape(blocked))

    part = (lines * chans, width_of)
    product, *sums = call(
        functools.partial(partial_kernel, split=split, scale=grad_scale, tile=512),
        [((4, rows, lines * chans), BF16)] + [(part, BF16)] * (4 * CHUNKS),
        (scalars, long_t, query_t, after(cot, d_long_t)),
        1,
        scratch=[pltpu.VMEM(flat, F32)],
        flops=1024,
    )
    d_gated_cols, filter_part = call(
        functools.partial(backward_kernel, scale=grad_scale, **sizes),
        [(blocked, BF16), ((chans, seq_len), BF16)],
        (d_long_cols, filt_spec, gated_cols, *tables),
        scratch=[work, signal, work],
        flops=3 * fft_flops,
    )
    (output,) = call(
        functools.partial(output_kernel, tile=512),
        [((rows, features), BF16)],
        (product, *weights),
        flops=2 * rows * width * features,
    )

    near_sum, over_sum, near_send, over_send = sums
    over_core, near_core = swap(over_send, "c"), swap(near_send, "c")
    over_sum = over_sum.astype(F32) + after(over_core, output).astype(F32)
    got = after(swap(over_sum.astype(BF16), "h"), filter_part)
    total = [
        near_sum[at].astype(F32) + near_core[at].astype(F32) + got[at].astype(F32)
        for at in (slice(i * chans, (i + 1) * chans) for i in range(lines))
    ]
    sent = [total[lines - step].astype(BF16) for step in range(1, lines)]
    filter_sum = dp_start(filter_part)
    total_here = after(total[0], *sent)
    for step, block in enumerate(sent, 1):
        total_here += lax.ppermute(block, "l", line_route(lines, step)).astype(F32)
    total_here = total_here.astype(BF16)
    d_wout = dp_finish(total_here, dp_start(total_here))

    d_gated_t = exchange(after(d_gated_cols, *sent)).reshape(flat)

    (head,) = call(
        functools.partial(head_kernel, width=width, split=split),
        [((8, 3 * width), F32)],
        inputs + (d_product_t, long_t, d_gated_t),
        1,
        flops=1 << 20,
    )
    d_filter = dp_finish(filter_part, after(filter_sum, head))
    later = lax.ppermute(head[:2], axes, [(j, i) for i, j in route])
    (d_proj,) = call(
        functools.partial(proj_grad_kernel, width=width, split=split),
        [((rows, 3 * width), BF16)],
        inputs + (d_product_t, long_t, d_gated_t, later),
        1,
        flops=1 << 20,
    )
    return output[None], d_proj[None], d_wout, d_filter


def solution(mesh):
    ctx, dp = mesh.shape["ctx"], mesh.shape["dp"]
    if ctx == 16:
        axes, dims = ("l", "h", "c"), (4, 2, 2)
    else:
        axes, dims = ("h", "l", "c"), (2, ctx // 4, 2)
    fine = Mesh(mesh.devices.reshape(dims + (dp,)), axes + ("dp",))
    placed = (
        P("dp", axes, None),
        P(),
        P(axes, None),
        P(axes, None),
        P("dp", axes, None),
        P(),
        P(),
    )
    return jax.shard_map(
        functools.partial(per_device, axes),
        mesh=fine,
        in_specs=placed,
        out_specs=(P("dp", axes, None), P("dp", axes, None), P(axes, None), P(axes, None)),
        check_vma=False,
    )
```

```python
import functools
import math
import typing

import jax
import jax.numpy as jnp
import ml_dtypes
import numpy as np
from jax import lax
from jax.experimental import pallas as pl
from jax.experimental.pallas import tpu as pltpu
from jax.sharding import Mesh
from jax.sharding import PartitionSpec as P

F32 = jnp.float32
BF16 = jnp.bfloat16
LANES = 128
VMEM_LIMIT = 8 << 20
SMEM = pl.BlockSpec(memory_space=pltpu.SMEM)


def split_bf16(values):
    high = values.astype(ml_dtypes.bfloat16)
    low = (values - high.astype(np.float64)).astype(ml_dtypes.bfloat16)
    return high, low


def fft_tables(blocks):
    size = 2 * blocks * LANES
    k1 = np.arange(blocks + 1)[:, None]
    lane = np.arange(LANES)
    angle = -2.0 * np.pi * (k1 * lane[None, :] % size) / size
    twist = np.stack([np.cos(angle), np.sin(angle)]).astype(np.float32)
    inner = -2.0 * np.pi * (lane[:, None] * lane[None, :] % LANES) / LANES
    cos, sin = np.cos(inner), np.sin(inner)
    matrix = np.block([[cos, sin], [-sin, cos]])
    high, low = split_bf16(matrix)
    return jnp.asarray(twist), jnp.asarray(np.stack([high, low]))


def real_fft(values):
    half = len(values)
    if half == 1:
        return [(values[0], None), (values[0], None)]
    even, odd = real_fft(values[0::2]), real_fft(values[1::2])
    out = [None] * (half + 1)
    out[0] = (even[0][0] + odd[0][0], None)
    out[half] = (even[0][0] - odd[0][0], None)
    out[half // 2] = (even[half // 2][0], -odd[half // 2][0])
    for k in range(1, half // 2):
        cos, sin = math.cos(math.pi * k / half), -math.sin(math.pi * k / half)
        (e_re, e_im), (o_re, o_im) = even[k], odd[k]
        t_re = o_re * cos - o_im * sin
        t_im = o_re * sin + o_im * cos
        out[k] = (e_re + t_re, e_im + t_im)
        out[half - k] = (e_re - t_re, t_im - e_im)
    return out


def real_ifft(spectrum):
    half = len(spectrum) - 1
    if half == 1:
        return [spectrum[0][0] + spectrum[1][0]]
    even = [None] * (half // 2 + 1)
    odd = [None] * (half // 2 + 1)
    even[0] = (spectrum[0][0] + spectrum[half][0], None)
    odd[0] = (spectrum[0][0] - spectrum[half][0], None)
    even[half // 2] = (2.0 * spectrum[half // 2][0], None)
    odd[half // 2] = (-2.0 * spectrum[half // 2][1], None)
    for k in range(1, half // 2):
        cos, sin = math.cos(math.pi * k / half), math.sin(math.pi * k / half)
        (a_re, a_im), (b_re, b_im) = spectrum[k], spectrum[half - k]
        even[k] = (a_re + b_re, a_im - b_im)
        d_re, d_im = a_re - b_re, a_im + b_im
        odd[k] = (d_re * cos - d_im * sin, d_re * sin + d_im * cos)
    out = [None] * half
    out[0::2] = real_ifft(even)
    out[1::2] = real_ifft(odd)
    return out


def split_dot(left, high, low, transposed):
    dims = (((1,), (1 if transposed else 0,)), ((), ()))
    dot = functools.partial(lax.dot_general, dimension_numbers=dims, preferred_element_type=F32)
    left_high = left.astype(BF16)
    left_low = (left - left_high.astype(F32)).astype(BF16)
    return dot(left_high, high) + (dot(left_low, high) + dot(left_high, low))


def to_spectrum(load, blocks, chans, twist, matrix, work):
    for first in range(0, chans, 8):
        rows = slice(first, first + 8)
        freqs = real_fft([load(n1, rows) for n1 in range(blocks)])
        for k1, (re, im) in enumerate(freqs):
            at = slice(k1 * chans + first, k1 * chans + first + 8)
            if k1 == 0:
                work[at, :LANES] = re
                work[at, LANES:] = jnp.zeros_like(re)
                continue
            cos, sin = twist[0, k1 : k1 + 1, :], twist[1, k1 : k1 + 1, :]
            if im is None:
                work[at, :LANES] = re * cos
                work[at, LANES:] = re * sin
            else:
                work[at, :LANES] = re * cos - im * sin
                work[at, LANES:] = re * sin + im * cos
    return split_dot(work[...], matrix[0], matrix[1], False)


def from_spectrum(spectrum, blocks, chans, twist, matrix, work, store):
    scale = 1.0 / (2 * blocks * LANES)
    work[...] = split_dot(spectrum, matrix[0], matrix[1], True)
    for first in range(0, chans, 8):
        rows = slice(first, first + 8)
        freqs = []
        for k1 in range(blocks + 1):
            at = slice(k1 * chans + first, k1 * chans + first + 8)
            re, im = work[at, :LANES] * scale, work[at, LANES:] * scale
            cos, sin = twist[0, k1 : k1 + 1, :], twist[1, k1 : k1 + 1, :]
            if k1 == 0:
                freqs.append((re, None))
            elif k1 == blocks:
                freqs.append((re * cos + im * sin, None))
            else:
                freqs.append((re * cos + im * sin, im * cos - re * sin))
        for n1, value in enumerate(real_ifft(freqs)):
            store(n1, rows, value)


def times(a, b):
    a_re, a_im, b_re, b_im = a[:, :LANES], a[:, LANES:], b[:, :LANES], b[:, LANES:]
    return jnp.concatenate([a_re * b_re - a_im * b_im, a_re * b_im + a_im * b_re], axis=1)


def conj_times(a, b):
    a_re, a_im, b_re, b_im = a[:, :LANES], a[:, LANES:], b[:, :LANES], b[:, LANES:]
    return jnp.concatenate([a_re * b_re + a_im * b_im, a_re * b_im - a_im * b_re], axis=1)


def filter_kernel(filt, twist, matrix, spec, work, *, blocks, chans):
    def load(n1, rows):
        return filt[rows, n1 * LANES : (n1 + 1) * LANES]

    spec[...] = to_spectrum(load, blocks, chans, twist, matrix, work)


def forward_kernel(
    gated, filt_spec, twist, matrix, long_out, work, signal, *, blocks, chans
):
    for n1 in range(blocks):
        signal[n1] = gated[n1].astype(F32)

    def load(n1, rows):
        return signal[n1, rows, :]

    spec = to_spectrum(load, blocks, chans, twist, matrix, work)

    def store(n1, rows, value):
        signal[n1, rows, :] = value

    from_spectrum(times(spec, filt_spec[...]), blocks, chans, twist, matrix, work, store)
    for n1 in range(blocks):
        long_out[n1] = signal[n1].astype(BF16)


def backward_kernel(
    d_long, filt_spec, twist, matrix, d_gated, work, signal, *, blocks, chans
):
    for n1 in range(blocks):
        signal[n1] = d_long[n1].astype(F32)

    def load(n1, rows):
        return signal[n1, rows, :]

    def store(n1, rows, value):
        signal[n1, rows, :] = value

    spec = conj_times(filt_spec[...], to_spectrum(load, blocks, chans, twist, matrix, work))
    from_spectrum(spec, blocks, chans, twist, matrix, work, store)
    for n1 in range(blocks):
        d_gated[n1] = signal[n1].astype(BF16)


def filter_grad_kernel(
    d_long, gated, twist, matrix, d_filter, work, signal, held, *, blocks, chans, scale
):
    def load(n1, rows):
        return signal[n1, rows, :]

    def store(n1, rows, value):
        signal[n1, rows, :] = value

    for n1 in range(blocks):
        signal[n1] = d_long[n1].astype(F32)
    held[...] = to_spectrum(load, blocks, chans, twist, matrix, work)
    for n1 in range(blocks):
        signal[n1] = gated[n1].astype(F32)
    spec = conj_times(to_spectrum(load, blocks, chans, twist, matrix, work), held[...])
    from_spectrum(spec, blocks, chans, twist, matrix, work, store)
    for n1 in range(blocks):
        d_filter[:, n1 * LANES : (n1 + 1) * LANES] = (signal[n1] * scale).astype(BF16)


class Split(typing.NamedTuple):
    samples: int
    lines: int
    chans: int
    line_first: bool


def mixed_stream(stream, proj, earlier, taps, room, width):
    rows = proj.shape[0]
    row = lax.broadcasted_iota(jnp.int32, (rows, 1), 0)
    past_row = lax.broadcasted_iota(jnp.int32, (2, 1), 0)
    cols = slice(stream * width, (stream + 1) * width)
    masked = jnp.where(row < room, proj[:, cols].astype(F32), 0.0)
    past = jnp.where(past_row < room + 2, earlier[:, cols].astype(F32), 0.0)
    mixed = taps[0:1, cols] * masked
    for tap in range(1, 3):
        shifted = pltpu.roll(masked, tap, 0)
        for r in range(tap):
            shifted = jnp.where(row == r, past[2 - tap + r : 3 - tap + r, :], shifted)
        mixed = mixed + taps[tap : tap + 1, cols] * shifted
    return mixed


def prep_kernel(scalars, proj, earlier, taps, gated_t, query_t, *, width, split):
    room = room_left(scalars, split, proj.shape[0])
    query, key, value = (
        mixed_stream(stream, proj, earlier, taps, room, width) for stream in range(3)
    )
    gated_t[...] = (key * value).T.astype(BF16)
    query_t[...] = query.T


def room_left(scalars, split, rows):
    group, sample = scalars[0] // split.samples, scalars[0] % split.samples
    length = scalars[1]
    for other in range(1, split.samples):
        length = jnp.where(sample == other, scalars[1 + other], length)
    return length - group * rows


def loss_weight(scalars, split):
    sample = scalars[0] % split.samples
    total, mine = jnp.float32(0), jnp.float32(0)
    for other in range(split.samples):
        count = scalars[1 + split.samples + other].astype(F32)
        total = total + count
        mine = jnp.where(sample == other, count, mine)
    return jnp.full((1, LANES), mine * split.samples) / jnp.full((1, LANES), total)


def natural_row(scalars, rel_h, rel_c, step, split):
    group = scalars[0] // split.samples
    lines, chans = split.lines, split.chans
    c = (group % 2 + rel_c) % 2
    if split.line_first:
        h, line = group // 2 % 2, group // 4
    else:
        h, line = group // (2 * lines), group // 2 % lines
    h, line = (h + rel_h) % 2, (line + lines - step) % lines
    at = (line * 2 + h) * 2 + c if split.line_first else (h * lines + line) * 2 + c
    return pl.multiple_of(at * chans, chans)


PIECES = ((0, 0), (1, 0), (0, 1), (1, 1))
CHUNKS = 1


def cotangent_kernel(scalars, dout, cot, *, split):
    rows = dout.shape[0]
    row = lax.broadcasted_iota(jnp.int32, (rows, 1), 0)
    mask = jnp.where(row < room_left(scalars, split, rows), 1.0, 0.0)
    weight = loss_weight(scalars, split)[:, :1]
    cot[...] = (dout[...].astype(F32) * mask * weight).astype(BF16)


def d_long_kernel(scalars, cot, query_t, *refs, split):
    *weights, d_product_t, d_long_t = refs
    lines, chans = split.lines, split.chans
    part = cot.shape[1] // CHUNKS
    for piece, (rel_h, rel_c) in enumerate(PIECES):
        got = sum(
            lax.dot_general(
                weights[piece * CHUNKS + chunk][...],
                cot[:, chunk * part : (chunk + 1) * part],
                (((1,), (1,)), ((), ())),
                preferred_element_type=F32,
            )
            for chunk in range(CHUNKS)
        )
        for line in range(lines):
            at = natural_row(scalars, rel_h, rel_c, line, split)
            d_product_t[pl.ds(at, chans), :] = got[line * chans : (line + 1) * chans]
    d_long_t[...] = (d_product_t[...] * query_t[...]).astype(BF16)


def partial_kernel(
    scalars, long_t, query_t, cot, product, *refs, split, scale, tile
):
    *parts, product_t = refs
    lines, chans = split.lines, split.chans
    part = cot.shape[1] // CHUNKS
    product_t[...] = query_t[...] * long_t[...].astype(F32)
    for piece, (rel_h, rel_c) in enumerate(PIECES):
        left = jnp.concatenate(
            [
                product_t[pl.ds(natural_row(scalars, rel_h, rel_c, line, split), chans), :]
                for line in range(lines)
            ],
            axis=0,
        )
        product[piece] = left.T.astype(BF16)
        left = left.astype(BF16)
        for first in range(0, cot.shape[1], tile):
            cols = slice(first, first + tile)
            got = jnp.dot(left, cot[:, cols], preferred_element_type=F32) * scale
            out = parts[(2 * rel_c + rel_h) * CHUNKS + first // part]
            out[:, first % part : first % part + tile] = got.astype(BF16)


def output_kernel(product, *refs, tile):
    *weights, out = refs
    part = out.shape[1] // CHUNKS
    for first in range(0, out.shape[1], tile):
        chunk, cols = first // part, slice(first % part, first % part + tile)
        total = sum(
            jnp.dot(
                product[piece], weights[piece * CHUNKS + chunk][:, cols], preferred_element_type=F32
            )
            for piece in range(4)
        )
        out[:, first : first + tile] = total.astype(BF16)


def mixed_grads(d_product_t, long_t, d_gated_t, key, value, rows):
    d_query = (d_product_t[...] * long_t[...].astype(F32)).T[:rows]
    d_gated = d_gated_t[...].astype(F32).T[:rows]
    return d_query, d_gated * value[:rows], d_gated * key[:rows]


def head_kernel(
    scalars, proj, earlier, taps, d_product_t, long_t, d_gated_t, head, *, width, split
):
    room = room_left(scalars, split, proj.shape[0])
    key, value = (mixed_stream(i, proj, earlier, taps, room, width) for i in (1, 2))
    grads = mixed_grads(d_product_t, long_t, d_gated_t, key, value, 8)
    for stream, grad in enumerate(grads):
        head[:, stream * width : (stream + 1) * width] = grad


def proj_grad_kernel(
    scalars,
    proj,
    earlier,
    taps,
    d_product_t,
    long_t,
    d_gated_t,
    later,
    d_proj,
    *,
    width,
    split,
):
    rows = proj.shape[0]
    row = lax.broadcasted_iota(jnp.int32, (rows, 1), 0)
    room = room_left(scalars, split, rows)
    key, value = (mixed_stream(i, proj, earlier, taps, room, width) for i in (1, 2))
    grads = mixed_grads(d_product_t, long_t, d_gated_t, key, value, rows)
    for stream, grad in enumerate(grads):
        cols = slice(stream * width, (stream + 1) * width)
        total = taps[0:1, cols] * grad
        for tap in range(1, 3):
            shifted = pltpu.roll(grad, rows - tap, 0)
            for r in range(tap):
                shifted = jnp.where(row == rows - tap + r, later[r : r + 1, cols], shifted)
            total = total + taps[tap : tap + 1, cols] * shifted
        d_proj[:, cols] = jnp.where(row < room, total, 0.0).astype(BF16)


def call(kernel, outs, args, scalars=0, scratch=(), flops=0, far=()):
    def full(value):
        return pl.BlockSpec(value.shape, lambda i, n=len(value.shape): (0,) * n)

    out_shape = [jax.ShapeDtypeStruct(shape, dtype) for shape, dtype in outs]
    return pl.pallas_call(
        kernel,
        grid=(1,),
        out_shape=out_shape,
        in_specs=[
            SMEM if i < scalars else HBM if i in far else full(v) for i, v in enumerate(args)
        ],
        out_specs=[full(v) for v in out_shape],
        scratch_shapes=list(scratch),
        compiler_params=pltpu.CompilerParams(vmem_limit_bytes=VMEM_LIMIT),
        cost_estimate=pl.CostEstimate(flops=flops, bytes_accessed=1024, transcendentals=0),
    )(*args)


SWAP = ((0, 1), (1, 0))


def after(value, *others):
    return lax.optimization_barrier((value,) + others)[0]


def swap(block, axis):
    return lax.ppermute(block, axis, SWAP)


def dp_start(block):
    return swap(block, "dp") if lax.axis_size("dp") == 2 else lax.psum(block, "dp")


def dp_finish(block, got):
    if lax.axis_size("dp") == 2:
        return block.astype(F32) + got.astype(F32)
    return got.astype(F32)


def line_route(lines, step):
    return [(i, (i + step) % lines) for i in range(lines)]


def along_line(block, lines):
    return [block] + [
        lax.ppermute(block, "l", line_route(lines, step)) for step in range(1, lines)
    ]


def per_device(axes, proj, short_filter, long_filter, w_out, dout, lengths, counts):
    rows, width = proj.shape[1], proj.shape[2] // 3
    chans, seq_len = long_filter.shape
    features = w_out.shape[1]
    batch = lengths.shape[0]
    ctx_size = seq_len // rows
    lines = lax.axis_size("l")
    split = Split(batch, lines, chans, axes[0] == "l")
    grad_scale = 1.0 / math.sqrt(batch * seq_len)
    assert batch == lax.axis_size("dp") and rows == LANES
    place = lax.axis_index(axes + ("dp",)).astype(jnp.int32).reshape(1)
    scalars = jnp.concatenate([place, lengths, counts])

    route = [(i, i + 1) for i in range(ctx_size - 1)]
    tail = proj[0, rows - 2 :]
    earlier = lax.ppermute(tail, axes, route)


    flat = (width, rows)
    width_of = features // CHUNKS
    parts = [
        along_line(after(w_out[:, i * width_of : (i + 1) * width_of], tail), lines)
        for i in range(CHUNKS)
    ]
    inputs = (scalars, proj[0], earlier, short_filter)
    gated_t, query_t = call(
        functools.partial(prep_kernel, width=width, split=split),
        [(flat, BF16), (flat, F32)],
        inputs,
        1,
        flops=1 << 20,
    )

    (cot,) = call(
        functools.partial(cotangent_kernel, split=split),
        [((rows, features), BF16)],
        (scalars, after(dout[0], gated_t)),
        1,
        flops=1 << 20,
    )

    def exchange(block):
        return lax.all_to_all(block, axes, 0, 0, tiled=True)

    blocked = (ctx_size, chans, rows)
    tables = fft_tables(ctx_size)
    spec_shape = ((ctx_size + 1) * chans, 2 * LANES)
    sizes = {"blocks": ctx_size, "chans": chans}
    work = pltpu.VMEM(spec_shape, F32)
    signal = pltpu.VMEM(blocked, F32)
    fft_flops = 6 * spec_shape[0] * 2 * LANES * 2 * LANES
    (filt_spec,) = call(
        functools.partial(filter_kernel, **sizes),
        [(spec_shape, F32)],
        (after(long_filter, gated_t), *tables),
        scratch=[work],
        flops=fft_flops,
    )
    near = [
        jnp.concatenate([after(part[0], filt_spec)] + part[1:]) for part in parts
    ]
    over = [swap(part, "h") for part in near]
    gated_cols = exchange(gated_t.reshape(blocked))
    (long_cols,) = call(
        functools.partial(forward_kernel, **sizes),
        [(blocked, BF16)],
        (gated_cols, filt_spec, *tables),
        scratch=[work, signal],
        flops=30 << 30,
    )
    long_t = exchange(long_cols).reshape(flat)
    over = [after(part, long_t) for part in over]
    weights = near + over + [swap(part, "c") for part in near + over]

    d_product_t, d_long_t = call(
        functools.partial(d_long_kernel, split=split),
        [(flat, F32), (flat, BF16)],
        (scalars, cot, query_t, *weights),
        1,
        flops=2 * rows * width * features,
    )
    d_long_cols = exchange(d_long_t.reshape(blocked))

    part = (lines * chans, width_of)
    product, *sums = call(
        functools.partial(partial_kernel, split=split, scale=grad_scale, tile=512),
        [((4, rows, lines * chans), BF16)] + [(part, BF16)] * (4 * CHUNKS),
        (scalars, long_t, query_t, after(cot, d_long_t)),
        1,
        scratch=[pltpu.VMEM(flat, F32)],
        flops=1024,
    )
    (d_gated_cols,) = call(
        functools.partial(backward_kernel, **sizes),
        [(blocked, BF16)],
        (d_long_cols, filt_spec, *tables),
        scratch=[work, signal],
        flops=2 * fft_flops,
    )
    (output,) = call(
        functools.partial(output_kernel, tile=512),
        [((rows, features), BF16)],
        (product, *weights),
        flops=2 * rows * width * features,
    )

    near_sum, over_sum, near_send, over_send = sums
    over_core, near_core = swap(over_send, "c"), swap(near_send, "c")
    over_sum = over_sum.astype(F32) + after(over_core, output).astype(F32)
    got = after(swap(over_sum.astype(BF16), "h"), d_gated_cols)
    total = [
        near_sum[at].astype(F32) + near_core[at].astype(F32) + got[at].astype(F32)
        for at in (slice(i * chans, (i + 1) * chans) for i in range(lines))
    ]
    sent = [total[lines - step].astype(BF16) for step in range(1, lines)]
    (filter_part,) = call(
        functools.partial(filter_grad_kernel, scale=grad_scale, **sizes),
        [((chans, seq_len), BF16)],
        (after(d_long_cols, *sent), gated_cols, *tables),
        scratch=[work, signal, work],
        flops=3 * fft_flops,
    )
    filter_sum = dp_start(filter_part)
    total_here = after(total[0], *sent)
    for step, block in enumerate(sent, 1):
        total_here += lax.ppermute(block, "l", line_route(lines, step)).astype(F32)
    total_here = total_here.astype(BF16)
    d_wout = dp_finish(total_here, dp_start(total_here))

    d_gated_t = exchange(after(d_gated_cols, *sent)).reshape(flat)

    (head,) = call(
        functools.partial(head_kernel, width=width, split=split),
        [((8, 3 * width), F32)],
        inputs + (d_product_t, long_t, d_gated_t),
        1,
        flops=1 << 20,
    )
    d_filter = dp_finish(filter_part, after(filter_sum, head))
    later = lax.ppermute(head[:2], axes, [(j, i) for i, j in route])
    (d_proj,) = call(
        functools.partial(proj_grad_kernel, width=width, split=split),
        [((rows, 3 * width), BF16)],
        inputs + (d_product_t, long_t, d_gated_t, later),
        1,
        flops=1 << 20,
    )
    return output[None], d_proj[None], d_wout, d_filter


def solution(mesh):
    ctx, dp = mesh.shape["ctx"], mesh.shape["dp"]
    if ctx == 16:
        axes, dims = ("l", "h", "c"), (4, 2, 2)
    else:
        axes, dims = ("h", "l", "c"), (2, ctx // 4, 2)
    fine = Mesh(mesh.devices.reshape(dims + (dp,)), axes + ("dp",))
    placed = (
        P("dp", axes, None),
        P(),
        P(axes, None),
        P(axes, None),
        P("dp", axes, None),
        P(),
        P(),
    )
    return jax.shard_map(
        functools.partial(per_device, axes),
        mesh=fine,
        in_specs=placed,
        out_specs=(P("dp", axes, None), P("dp", axes, None), P(axes, None), P(axes, None)),
        check_vma=False,
    )
```

```python
import functools
import math
import typing

import jax
import jax.numpy as jnp
import ml_dtypes
import numpy as np
from jax import lax
from jax.experimental import pallas as pl
from jax.experimental.pallas import tpu as pltpu
from jax.sharding import Mesh
from jax.sharding import PartitionSpec as P

F32 = jnp.float32
BF16 = jnp.bfloat16
LANES = 128
VMEM_LIMIT = 8 << 20
SMEM = pl.BlockSpec(memory_space=pltpu.SMEM)


def split_bf16(values):
    high = values.astype(ml_dtypes.bfloat16)
    low = (values - high.astype(np.float64)).astype(ml_dtypes.bfloat16)
    return high, low


def fft_tables(blocks):
    size = 2 * blocks * LANES
    k1 = np.arange(blocks + 1)[:, None]
    lane = np.arange(LANES)
    angle = -2.0 * np.pi * (k1 * lane[None, :] % size) / size
    twist = np.stack([np.cos(angle), np.sin(angle)]).astype(np.float32)
    inner = -2.0 * np.pi * (lane[:, None] * lane[None, :] % LANES) / LANES
    cos, sin = np.cos(inner), np.sin(inner)
    matrix = np.block([[cos, sin], [-sin, cos]])
    high, low = split_bf16(matrix)
    return jnp.asarray(twist), jnp.asarray(np.stack([high, low]))


def real_fft(values):
    half = len(values)
    if half == 1:
        return [(values[0], None), (values[0], None)]
    even, odd = real_fft(values[0::2]), real_fft(values[1::2])
    out = [None] * (half + 1)
    out[0] = (even[0][0] + odd[0][0], None)
    out[half] = (even[0][0] - odd[0][0], None)
    out[half // 2] = (even[half // 2][0], -odd[half // 2][0])
    for k in range(1, half // 2):
        cos, sin = math.cos(math.pi * k / half), -math.sin(math.pi * k / half)
        (e_re, e_im), (o_re, o_im) = even[k], odd[k]
        t_re = o_re * cos - o_im * sin
        t_im = o_re * sin + o_im * cos
        out[k] = (e_re + t_re, e_im + t_im)
        out[half - k] = (e_re - t_re, t_im - e_im)
    return out


def real_ifft(spectrum):
    half = len(spectrum) - 1
    if half == 1:
        return [spectrum[0][0] + spectrum[1][0]]
    even = [None] * (half // 2 + 1)
    odd = [None] * (half // 2 + 1)
    even[0] = (spectrum[0][0] + spectrum[half][0], None)
    odd[0] = (spectrum[0][0] - spectrum[half][0], None)
    even[half // 2] = (2.0 * spectrum[half // 2][0], None)
    odd[half // 2] = (-2.0 * spectrum[half // 2][1], None)
    for k in range(1, half // 2):
        cos, sin = math.cos(math.pi * k / half), math.sin(math.pi * k / half)
        (a_re, a_im), (b_re, b_im) = spectrum[k], spectrum[half - k]
        even[k] = (a_re + b_re, a_im - b_im)
        d_re, d_im = a_re - b_re, a_im + b_im
        odd[k] = (d_re * cos - d_im * sin, d_re * sin + d_im * cos)
    out = [None] * half
    out[0::2] = real_ifft(even)
    out[1::2] = real_ifft(odd)
    return out


def split_dot(left, high, low, transposed):
    dims = (((1,), (1 if transposed else 0,)), ((), ()))
    dot = functools.partial(lax.dot_general, dimension_numbers=dims, preferred_element_type=F32)
    left_high = left.astype(BF16)
    left_low = (left - left_high.astype(F32)).astype(BF16)
    return dot(left_high, high) + (dot(left_low, high) + dot(left_high, low))


def to_spectrum(load, blocks, chans, twist, matrix, work):
    for first in range(0, chans, 8):
        rows = slice(first, first + 8)
        freqs = real_fft([load(n1, rows) for n1 in range(blocks)])
        for k1, (re, im) in enumerate(freqs):
            at = slice(k1 * chans + first, k1 * chans + first + 8)
            if k1 == 0:
                work[at, :LANES] = re
                work[at, LANES:] = jnp.zeros_like(re)
                continue
            cos, sin = twist[0, k1 : k1 + 1, :], twist[1, k1 : k1 + 1, :]
            if im is None:
                work[at, :LANES] = re * cos
                work[at, LANES:] = re * sin
            else:
                work[at, :LANES] = re * cos - im * sin
                work[at, LANES:] = re * sin + im * cos
    return split_dot(work[...], matrix[0], matrix[1], False)


def from_spectrum(spectrum, blocks, chans, twist, matrix, work, store):
    scale = 1.0 / (2 * blocks * LANES)
    work[...] = split_dot(spectrum, matrix[0], matrix[1], True)
    for first in range(0, chans, 8):
        rows = slice(first, first + 8)
        freqs = []
        for k1 in range(blocks + 1):
            at = slice(k1 * chans + first, k1 * chans + first + 8)
            re, im = work[at, :LANES] * scale, work[at, LANES:] * scale
            cos, sin = twist[0, k1 : k1 + 1, :], twist[1, k1 : k1 + 1, :]
            if k1 == 0:
                freqs.append((re, None))
            elif k1 == blocks:
                freqs.append((re * cos + im * sin, None))
            else:
                freqs.append((re * cos + im * sin, im * cos - re * sin))
        for n1, value in enumerate(real_ifft(freqs)):
            store(n1, rows, value)


def times(a, b):
    a_re, a_im, b_re, b_im = a[:, :LANES], a[:, LANES:], b[:, :LANES], b[:, LANES:]
    return jnp.concatenate([a_re * b_re - a_im * b_im, a_re * b_im + a_im * b_re], axis=1)


def conj_times(a, b):
    a_re, a_im, b_re, b_im = a[:, :LANES], a[:, LANES:], b[:, :LANES], b[:, LANES:]
    return jnp.concatenate([a_re * b_re + a_im * b_im, a_re * b_im - a_im * b_re], axis=1)


def filter_kernel(filt, twist, matrix, spec, work, *, blocks, chans):
    def load(n1, rows):
        return filt[rows, n1 * LANES : (n1 + 1) * LANES]

    spec[...] = to_spectrum(load, blocks, chans, twist, matrix, work)


def forward_kernel(
    gated, filt_spec, twist, matrix, long_out, work, signal, *, blocks, chans
):
    for n1 in range(blocks):
        signal[n1] = gated[n1].astype(F32)

    def load(n1, rows):
        return signal[n1, rows, :]

    spec = to_spectrum(load, blocks, chans, twist, matrix, work)

    def store(n1, rows, value):
        signal[n1, rows, :] = value

    from_spectrum(times(spec, filt_spec[...]), blocks, chans, twist, matrix, work, store)
    for n1 in range(blocks):
        long_out[n1] = signal[n1].astype(BF16)


def backward_kernel(
    d_long, filt_spec, twist, matrix, d_gated, work, signal, *, blocks, chans
):
    for n1 in range(blocks):
        signal[n1] = d_long[n1].astype(F32)

    def load(n1, rows):
        return signal[n1, rows, :]

    def store(n1, rows, value):
        signal[n1, rows, :] = value

    spec = conj_times(filt_spec[...], to_spectrum(load, blocks, chans, twist, matrix, work))
    from_spectrum(spec, blocks, chans, twist, matrix, work, store)
    for n1 in range(blocks):
        d_gated[n1] = signal[n1].astype(BF16)


def filter_grad_kernel(
    d_long, gated, twist, matrix, d_filter, work, signal, held, *, blocks, chans, scale
):
    def load(n1, rows):
        return signal[n1, rows, :]

    def store(n1, rows, value):
        signal[n1, rows, :] = value

    for n1 in range(blocks):
        signal[n1] = d_long[n1].astype(F32)
    held[...] = to_spectrum(load, blocks, chans, twist, matrix, work)
    for n1 in range(blocks):
        signal[n1] = gated[n1].astype(F32)
    spec = conj_times(to_spectrum(load, blocks, chans, twist, matrix, work), held[...])
    from_spectrum(spec, blocks, chans, twist, matrix, work, store)
    for n1 in range(blocks):
        d_filter[:, n1 * LANES : (n1 + 1) * LANES] = (signal[n1] * scale).astype(BF16)


class Split(typing.NamedTuple):
    samples: int
    lines: int
    chans: int
    line_first: bool


def mixed_stream(stream, proj, earlier, taps, room, width):
    rows = proj.shape[0]
    row = lax.broadcasted_iota(jnp.int32, (rows, 1), 0)
    past_row = lax.broadcasted_iota(jnp.int32, (2, 1), 0)
    cols = slice(stream * width, (stream + 1) * width)
    masked = jnp.where(row < room, proj[:, cols].astype(F32), 0.0)
    past = jnp.where(past_row < room + 2, earlier[:, cols].astype(F32), 0.0)
    mixed = taps[0:1, cols] * masked
    for tap in range(1, 3):
        shifted = pltpu.roll(masked, tap, 0)
        for r in range(tap):
            shifted = jnp.where(row == r, past[2 - tap + r : 3 - tap + r, :], shifted)
        mixed = mixed + taps[tap : tap + 1, cols] * shifted
    return mixed


def prep_kernel(scalars, proj, earlier, taps, gated_t, query_t, *, width, split):
    room = room_left(scalars, split, proj.shape[0])
    query, key, value = (
        mixed_stream(stream, proj, earlier, taps, room, width) for stream in range(3)
    )
    gated_t[...] = (key * value).T.astype(BF16)
    query_t[...] = query.T


def room_left(scalars, split, rows):
    group, sample = scalars[0] // split.samples, scalars[0] % split.samples
    length = scalars[1]
    for other in range(1, split.samples):
        length = jnp.where(sample == other, scalars[1 + other], length)
    return length - group * rows


def loss_weight(scalars, split):
    sample = scalars[0] % split.samples
    total, mine = jnp.float32(0), jnp.float32(0)
    for other in range(split.samples):
        count = scalars[1 + split.samples + other].astype(F32)
        total = total + count
        mine = jnp.where(sample == other, count, mine)
    return jnp.full((1, LANES), mine * split.samples) / jnp.full((1, LANES), total)


def natural_row(scalars, rel_h, rel_c, step, split):
    group = scalars[0] // split.samples
    lines, chans = split.lines, split.chans
    c = (group % 2 + rel_c) % 2
    if split.line_first:
        h, line = group // 2 % 2, group // 4
    else:
        h, line = group // (2 * lines), group // 2 % lines
    h, line = (h + rel_h) % 2, (line + lines - step) % lines
    at = (line * 2 + h) * 2 + c if split.line_first else (h * lines + line) * 2 + c
    return pl.multiple_of(at * chans, chans)


PIECES = ((0, 0), (1, 0), (0, 1), (1, 1))
CHUNKS = 1


def cotangent_kernel(scalars, dout, cot, *, split):
    rows = dout.shape[0]
    row = lax.broadcasted_iota(jnp.int32, (rows, 1), 0)
    mask = jnp.where(row < room_left(scalars, split, rows), 1.0, 0.0)
    weight = loss_weight(scalars, split)[:, :1]
    cot[...] = (dout[...].astype(F32) * mask * weight).astype(BF16)


def d_long_kernel(scalars, cot, query_t, *refs, split):
    *weights, d_product_t, d_long_t = refs
    lines, chans = split.lines, split.chans
    part = cot.shape[1] // CHUNKS
    for piece, (rel_h, rel_c) in enumerate(PIECES):
        got = sum(
            lax.dot_general(
                weights[piece * CHUNKS + chunk][...],
                cot[:, chunk * part : (chunk + 1) * part],
                (((1,), (1,)), ((), ())),
                preferred_element_type=F32,
            )
            for chunk in range(CHUNKS)
        )
        for line in range(lines):
            at = natural_row(scalars, rel_h, rel_c, line, split)
            d_product_t[pl.ds(at, chans), :] = got[line * chans : (line + 1) * chans]
    d_long_t[...] = (d_product_t[...] * query_t[...]).astype(BF16)


def partial_kernel(
    scalars, long_t, query_t, cot, product, *refs, split, scale, tile
):
    *parts, product_t = refs
    lines, chans = split.lines, split.chans
    part = cot.shape[1] // CHUNKS
    product_t[...] = query_t[...] * long_t[...].astype(F32)
    for piece, (rel_h, rel_c) in enumerate(PIECES):
        left = jnp.concatenate(
            [
                product_t[pl.ds(natural_row(scalars, rel_h, rel_c, line, split), chans), :]
                for line in range(lines)
            ],
            axis=0,
        )
        product[piece] = left.T.astype(BF16)
        left = left.astype(BF16)
        for first in range(0, cot.shape[1], tile):
            cols = slice(first, first + tile)
            got = jnp.dot(left, cot[:, cols], preferred_element_type=F32) * scale
            out = parts[(2 * rel_c + rel_h) * CHUNKS + first // part]
            out[:, first % part : first % part + tile] = got.astype(BF16)


def output_kernel(product, *refs, tile):
    *weights, out = refs
    part = out.shape[1] // CHUNKS
    for first in range(0, out.shape[1], tile):
        chunk, cols = first // part, slice(first % part, first % part + tile)
        total = sum(
            jnp.dot(
                product[piece], weights[piece * CHUNKS + chunk][:, cols], preferred_element_type=F32
            )
            for piece in range(4)
        )
        out[:, first : first + tile] = total.astype(BF16)


def mixed_grads(d_product_t, long_t, d_gated_t, key, value, rows):
    d_query = (d_product_t[...] * long_t[...].astype(F32)).T[:rows]
    d_gated = d_gated_t[...].astype(F32).T[:rows]
    return d_query, d_gated * value[:rows], d_gated * key[:rows]


def head_kernel(
    scalars, proj, earlier, taps, d_product_t, long_t, d_gated_t, head, *, width, split
):
    room = room_left(scalars, split, proj.shape[0])
    key, value = (mixed_stream(i, proj, earlier, taps, room, width) for i in (1, 2))
    grads = mixed_grads(d_product_t, long_t, d_gated_t, key, value, 8)
    for stream, grad in enumerate(grads):
        head[:, stream * width : (stream + 1) * width] = grad


def proj_grad_kernel(
    scalars,
    proj,
    earlier,
    taps,
    d_product_t,
    long_t,
    d_gated_t,
    later,
    d_proj,
    *,
    width,
    split,
):
    rows = proj.shape[0]
    row = lax.broadcasted_iota(jnp.int32, (rows, 1), 0)
    room = room_left(scalars, split, rows)
    key, value = (mixed_stream(i, proj, earlier, taps, room, width) for i in (1, 2))
    grads = mixed_grads(d_product_t, long_t, d_gated_t, key, value, rows)
    for stream, grad in enumerate(grads):
        cols = slice(stream * width, (stream + 1) * width)
        total = taps[0:1, cols] * grad
        for tap in range(1, 3):
            shifted = pltpu.roll(grad, rows - tap, 0)
            for r in range(tap):
                shifted = jnp.where(row == rows - tap + r, later[r : r + 1, cols], shifted)
            total = total + taps[tap : tap + 1, cols] * shifted
        d_proj[:, cols] = jnp.where(row < room, total, 0.0).astype(BF16)


def call(kernel, outs, args, scalars=0, scratch=(), flops=0, far=()):
    def full(value):
        return pl.BlockSpec(value.shape, lambda i, n=len(value.shape): (0,) * n)

    out_shape = [jax.ShapeDtypeStruct(shape, dtype) for shape, dtype in outs]
    return pl.pallas_call(
        kernel,
        grid=(1,),
        out_shape=out_shape,
        in_specs=[
            SMEM if i < scalars else HBM if i in far else full(v) for i, v in enumerate(args)
        ],
        out_specs=[full(v) for v in out_shape],
        scratch_shapes=list(scratch),
        compiler_params=pltpu.CompilerParams(vmem_limit_bytes=VMEM_LIMIT),
        cost_estimate=pl.CostEstimate(flops=flops, bytes_accessed=1024, transcendentals=0),
    )(*args)


SWAP = ((0, 1), (1, 0))


def after(value, *others):
    return lax.optimization_barrier((value,) + others)[0]


def swap(block, axis):
    return lax.ppermute(block, axis, SWAP)


def dp_start(block):
    return swap(block, "dp") if lax.axis_size("dp") == 2 else lax.psum(block, "dp")


def dp_finish(block, got):
    if lax.axis_size("dp") == 2:
        return block.astype(F32) + got.astype(F32)
    return got.astype(F32)


def line_route(lines, step):
    return [(i, (i + step) % lines) for i in range(lines)]


def along_line(block, lines):
    return [block] + [
        lax.ppermute(block, "l", line_route(lines, step)) for step in range(1, lines)
    ]


def per_device(axes, proj, short_filter, long_filter, w_out, dout, lengths, counts):
    rows, width = proj.shape[1], proj.shape[2] // 3
    chans, seq_len = long_filter.shape
    features = w_out.shape[1]
    batch = lengths.shape[0]
    ctx_size = seq_len // rows
    lines = lax.axis_size("l")
    split = Split(batch, lines, chans, axes[0] == "l")
    grad_scale = 1.0 / math.sqrt(batch * seq_len)
    assert batch == lax.axis_size("dp") and rows == LANES
    place = lax.axis_index(axes + ("dp",)).astype(jnp.int32).reshape(1)
    scalars = jnp.concatenate([place, lengths, counts])

    route = [(i, i + 1) for i in range(ctx_size - 1)]
    tail = proj[0, rows - 2 :]
    earlier = lax.ppermute(tail, axes, route)


    flat = (width, rows)
    width_of = features // CHUNKS
    parts = [
        along_line(after(w_out[:, i * width_of : (i + 1) * width_of], tail), lines)
        for i in range(CHUNKS)
    ]
    inputs = (scalars, proj[0], earlier, short_filter)
    gated_t, query_t = call(
        functools.partial(prep_kernel, width=width, split=split),
        [(flat, BF16), (flat, F32)],
        inputs,
        1,
        flops=1 << 20,
    )

    (cot,) = call(
        functools.partial(cotangent_kernel, split=split),
        [((rows, features), BF16)],
        (scalars, after(dout[0], gated_t)),
        1,
        flops=1 << 20,
    )

    def exchange(block):
        return lax.all_to_all(block, axes, 0, 0, tiled=True)

    blocked = (ctx_size, chans, rows)
    tables = fft_tables(ctx_size)
    spec_shape = ((ctx_size + 1) * chans, 2 * LANES)
    sizes = {"blocks": ctx_size, "chans": chans}
    work = pltpu.VMEM(spec_shape, F32)
    signal = pltpu.VMEM(blocked, F32)
    fft_flops = 6 * spec_shape[0] * 2 * LANES * 2 * LANES
    (filt_spec,) = call(
        functools.partial(filter_kernel, **sizes),
        [(spec_shape, F32)],
        (after(long_filter, gated_t), *tables),
        scratch=[work],
        flops=fft_flops,
    )
    near = [
        jnp.concatenate([after(part[0], filt_spec)] + part[1:]) for part in parts
    ]
    over = [swap(part, "h") for part in near]
    gated_cols = exchange(gated_t.reshape(blocked))
    (long_cols,) = call(
        functools.partial(forward_kernel, **sizes),
        [(blocked, BF16)],
        (gated_cols, filt_spec, *tables),
        scratch=[work, signal],
        flops=30 << 30,
    )
    long_t = exchange(long_cols).reshape(flat)
    over = [after(part, long_t) for part in over]
    weights = near + over + [swap(part, "c") for part in near + over]

    d_product_t, d_long_t = call(
        functools.partial(d_long_kernel, split=split),
        [(flat, F32), (flat, BF16)],
        (scalars, cot, query_t, *weights),
        1,
        flops=2 * rows * width * features,
    )
    d_long_cols = exchange(d_long_t.reshape(blocked))

    part = (lines * chans, width_of)
    product, *sums = call(
        functools.partial(partial_kernel, split=split, scale=grad_scale, tile=512),
        [((4, rows, lines * chans), BF16)] + [(part, BF16)] * (4 * CHUNKS),
        (scalars, long_t, query_t, after(cot, *weights)),
        1,
        scratch=[pltpu.VMEM(flat, F32)],
        flops=1024,
    )
    (d_gated_cols,) = call(
        functools.partial(backward_kernel, **sizes),
        [(blocked, BF16)],
        (d_long_cols, filt_spec, *tables),
        scratch=[work, signal],
        flops=2 * fft_flops,
    )
    (output,) = call(
        functools.partial(output_kernel, tile=512),
        [((rows, features), BF16)],
        (product, *weights),
        flops=2 * rows * width * features,
    )

    near_sum, over_sum, near_send, over_send = sums
    over_core, near_core = swap(over_send, "c"), swap(near_send, "c")
    over_sum = over_sum.astype(F32) + after(over_core, output).astype(F32)
    got = after(swap(over_sum.astype(BF16), "h"), d_gated_cols)
    total = [
        near_sum[at].astype(F32) + near_core[at].astype(F32) + got[at].astype(F32)
        for at in (slice(i * chans, (i + 1) * chans) for i in range(lines))
    ]
    sent = [total[lines - step].astype(BF16) for step in range(1, lines)]
    (filter_part,) = call(
        functools.partial(filter_grad_kernel, scale=grad_scale, **sizes),
        [((chans, seq_len), BF16)],
        (after(d_long_cols, *sent), gated_cols, *tables),
        scratch=[work, signal, work],
        flops=3 * fft_flops,
    )
    filter_sum = dp_start(filter_part)
    total_here = after(total[0], *sent)
    for step, block in enumerate(sent, 1):
        total_here += lax.ppermute(block, "l", line_route(lines, step)).astype(F32)
    total_here = total_here.astype(BF16)
    d_wout = dp_finish(total_here, dp_start(total_here))

    d_gated_t = exchange(after(d_gated_cols, *sent)).reshape(flat)

    (head,) = call(
        functools.partial(head_kernel, width=width, split=split),
        [((8, 3 * width), F32)],
        inputs + (d_product_t, long_t, d_gated_t),
        1,
        flops=1 << 20,
    )
    d_filter = dp_finish(filter_part, after(filter_sum, head))
    later = lax.ppermute(head[:2], axes, [(j, i) for i, j in route])
    (d_proj,) = call(
        functools.partial(proj_grad_kernel, width=width, split=split),
        [((rows, 3 * width), BF16)],
        inputs + (d_product_t, long_t, d_gated_t, later),
        1,
        flops=1 << 20,
    )
    return output[None], d_proj[None], d_wout, d_filter


def solution(mesh):
    ctx, dp = mesh.shape["ctx"], mesh.shape["dp"]
    if ctx == 16:
        axes, dims = ("l", "h", "c"), (4, 2, 2)
    else:
        axes, dims = ("h", "l", "c"), (2, ctx // 4, 2)
    fine = Mesh(mesh.devices.reshape(dims + (dp,)), axes + ("dp",))
    placed = (
        P("dp", axes, None),
        P(),
        P(axes, None),
        P(axes, None),
        P("dp", axes, None),
        P(),
        P(),
    )
    return jax.shard_map(
        functools.partial(per_device, axes),
        mesh=fine,
        in_specs=placed,
        out_specs=(P("dp", axes, None), P("dp", axes, None), P(axes, None), P(axes, None)),
        check_vma=False,
    )
```
